32 devices in a mesh: head: 2 (over x), ctx: 16 (over z, y, core).
Axes of the slice: x: 2, y: 2, z: 4, core: 2. Of those that a mesh axis runs over, the one named last changes fastest.
Arguments:
- queries: bfloat16 [2048, 1024], P(('head', 'ctx')), may hold values from -30 to 30
- key_vecs: bfloat16 [2048, 128], P(('head', 'ctx')), may hold values from -10 to 10
- value_vecs: bfloat16 [2048, 128], P(('head', 'ctx')), may hold values from -6 to 6
- out_grad: bfloat16 [2048, 1024], P(('head', 'ctx')), may hold values from -6 to 6
- positions: int32 [2048], P(('head', 'ctx')), may hold values from 0 to 2047, as said below
- documents: int32 [2048], P(('head', 'ctx')), may hold values from 0 to 2, as said below
Outputs:
- grad_queries: float32 [2048, 1024], P(('head', 'ctx'))
- grad_keys: float32 [2048, 128], P(('head', 'ctx'))
- grad_values: float32 [2048, 128], P(('head', 'ctx'))
The draws below stay inside these ranges and needn't reach their ends.
Inputs may be any that keep to these rules, and one draw needn't show every extreme that they name: positions is a permutation of 0 to 2047; each aligned run of 64 rows holds 64 consecutive positions in rising order. `documents`: document ids never fall as positions rise, the token at position 0 has id 0, and every id up to the most occurs.
All inputs are finite; a program needn't handle non-finite values.
Results may differ from the reference program's by a relative error of at most 0.0059.
Values may be sent and summed in bfloat16 or wider, within the bound.
A program may use at most 64 MiB of HBM per device.

```python
import math
import jax
import jax.numpy as jnp
from jax import lax

HD = 128
HEADS = 8
SEQ = 2048
RUN_LEN = 64


def draw_queries(key, part):
    sample = 1.5 * jnp.clip(jax.random.normal(jax.random.fold_in(key, 1), (SEQ, HEADS, HD), jnp.float32), -4.0, 4.0)
    return sample.reshape(SEQ, HEADS * HD).astype(jnp.bfloat16)


def draw_key_vecs(key, part):
    sample = jnp.clip(jax.random.normal(jax.random.fold_in(key, 2), (SEQ, HD), jnp.float32), -4.0, 4.0)
    return sample.astype(jnp.bfloat16)


def draw_positions(key, part):
    run_count = SEQ // RUN_LEN
    order = jax.random.permutation(jax.random.fold_in(key, 11), run_count).astype(jnp.int32)
    row_ids = jnp.arange(SEQ, dtype=jnp.int32)
    return (order[row_ids // RUN_LEN] * RUN_LEN + row_ids % RUN_LEN).astype(jnp.int32)


def draw_documents(key, part):
    placed = draw_positions(key, part)
    start_count = max(SEQ // 1024, 2)
    shuffled = jax.random.permutation(jax.random.fold_in(key, 13), SEQ - 1).astype(jnp.int32) + 1
    chosen = shuffled[:start_count]
    starts = jnp.zeros((SEQ,), jnp.int32).at[chosen].set(1)
    doc_at_position = jnp.cumsum(starts).astype(jnp.int32)
    return doc_at_position[placed].astype(jnp.int32)


def levels(rng, extent, split, least, top_value):
    gain = 1.0
    for position, parts in split:
        heights = jax.random.uniform(jax.random.fold_in(jax.random.fold_in(rng, 6), position), (parts,), jnp.float32, least / len(split), top_value / len(split))
        gain = gain * jnp.repeat(jnp.exp(heights), extent[position] // parts).reshape((-1,) + (1,) * (len(extent) - 1 - position))
    return gain


def normal_values(rng, extent, scale, most, shards=(), kind=jnp.bfloat16):
    drawn = scale * jax.random.normal(rng, extent, jnp.float32)
    if shards:
        drawn = drawn * levels(rng, extent, shards, -0.22, 0.18)
    return jnp.clip(drawn, -most, most).astype(kind)


def setup_inputs(seed: int = 0) -> dict:
    key_list = jax.random.split(jax.random.key(seed), 7)
    queries = draw_queries(jax.random.fold_in(key_list[6], 71), 0)
    key_vecs = draw_key_vecs(jax.random.fold_in(key_list[6], 71), 0)
    value_vecs = normal_values(key_list[2], (SEQ, HD), 1.0, 6.0, ((0, 32),))
    out_grad = normal_values(key_list[3], (SEQ, HEADS * HD), 1.0, 6.0, ((0, 32),))
    positions = draw_positions(jax.random.fold_in(key_list[6], 71), 0)
    documents = draw_documents(jax.random.fold_in(key_list[6], 71), 0)
    return {"queries": queries, "key_vecs": key_vecs, "value_vecs": value_vecs, "out_grad": out_grad, "positions": positions, "documents": documents}


NEG_BIG = -1e+30

def reference(queries, key_vecs, value_vecs, out_grad, positions, documents):
    seq_len = queries.shape[0]
    head_count = queries.shape[1] // HD
    inv_root = 1.0 / math.sqrt(HD)
    query_cube = queries.astype(jnp.float32).reshape(seq_len, head_count, HD)
    grad_cube = out_grad.astype(jnp.float32).reshape(seq_len, head_count, HD)
    key_full = key_vecs.astype(jnp.float32)
    value_full = value_vecs.astype(jnp.float32)
    block_len = 128
    block_count = seq_len // block_len

    def visit(running, block_index):
        key_acc, value_acc = running
        offset = (block_index * block_len).astype(jnp.int32)
        query_block = lax.dynamic_slice_in_dim(query_cube, offset, block_len, 0)
        grad_block = lax.dynamic_slice_in_dim(grad_cube, offset, block_len, 0)
        pos_query = lax.dynamic_slice_in_dim(positions, offset, block_len, 0)
        doc_query = lax.dynamic_slice_in_dim(documents, offset, block_len, 0)
        visible = (positions[None, :] <= pos_query[:, None]) & (documents[None, :] == doc_query[:, None])
        visible3 = visible[:, None, :]
        scores = jnp.where(visible3, jnp.einsum('thd,kd->thk', query_block, key_full) * inv_root, NEG_BIG)
        highest = lax.optimization_barrier(jnp.max(scores, axis=2))
        denoms = lax.optimization_barrier(jnp.sum(jnp.where(visible3, jnp.exp(scores - highest[:, :, None]), 0.0), axis=2))
        log_total = highest + jnp.log(denoms)
        weights = jnp.where(visible3, jnp.exp(scores - log_total[:, :, None]), 0.0)
        dprobs = jnp.einsum('thd,kd->thk', grad_block, value_full)
        row_dot = lax.optimization_barrier(jnp.sum(weights * dprobs, axis=2))
        dscores = lax.optimization_barrier((weights * (dprobs - row_dot[:, :, None])).astype(jnp.bfloat16)).astype(jnp.float32)
        weights_b = lax.optimization_barrier(weights.astype(jnp.bfloat16)).astype(jnp.float32)
        query_part = jnp.einsum('thk,kd->thd', dscores, key_full) * inv_root
        key_acc = key_acc + jnp.einsum('thk,thd->kd', dscores, query_block) * inv_root
        value_acc = value_acc + jnp.einsum('thk,thd->kd', weights_b, grad_block)
        return ((key_acc, value_acc), query_part)
    zero_rows = jnp.zeros((seq_len, HD), jnp.float32)
    (grad_keys, grad_values), query_parts = lax.scan(visit, (zero_rows, zero_rows), jnp.arange(block_count, dtype=jnp.int32))
    grad_queries = query_parts.reshape(seq_len, head_count * HD)
    return (grad_queries, grad_keys, grad_values)
```

```python
import functools
import math

import jax
import jax.numpy as jnp
from jax import lax
from jax.experimental import pallas as pl
from jax.experimental.pallas import tpu as pltpu
from jax.sharding import PartitionSpec as P

MESH = pl.DeviceIdType.MESH
NEG_BIG = -1e30
CORES = 2
SIDES = 2
F32 = jnp.float32
BF16 = jnp.bfloat16


def dot(lhs, rhs, lhs_dim, rhs_dim):
    return lax.dot_general(
        lhs, rhs, (((lhs_dim,), (rhs_dim,)), ((), ())), preferred_element_type=F32
    )


def kernel(
    cfg,
    q_ref, k_ref, v_ref, g_ref, pos_ref, doc_ref,
    dq_ref, dk_ref, dv_ref,
    qs, gs, kv, info, sbuf, dpbuf, top, den, cross, dqt, acck, accv,
    core_out, core_in, yk_out, yk_in, xv_out, xv_in, xk_out, xk_in, yv_out, yv_in,
    a_out, a_in, a_own, *sems,
):
    nx, na, rows, heads, docs = cfg
    chunk = na * rows
    lanes = heads * rows
    half = SIDES * nx
    inv_root = 1.0 / math.sqrt(128)
    scale = inv_root * math.log2(math.e)

    x = lax.axis_index("head")
    ctx = lax.axis_index("ctx")
    a, y, c = ctx // 4, (ctx // 2) % 2, ctx % 2

    def device(a_=None, y_=None, c_=None, x_=None):
        a_ = a if a_ is None else a_
        y_ = y if y_ is None else y_
        c_ = c if c_ is None else c_
        return (x if x_ is None else x_, a_ * 4 + y_ * 2 + c_)

    a_peers = [device(a_=(a + r) % na) for r in range(1, na)]
    x_peers = [device(x_=(x + r) % nx) for r in range(1, nx)]
    y_peer = device(y_=1 - y)
    c_peer = device(c_=1 - c)

    (s_akv, r_akv, s_ainf, r_ainf, s_xkv, r_xkv, s_xinf, r_xinf, s_ykv, r_ykv, s_yinf, r_yinf,
     s_fk, r_fk, s_finf, r_finf, s_fv, r_fv, s_ckv, r_ckv, s_cinf, r_cinf,
     s_rc, r_rc, s_k1, r_k1, s_v1, r_v1, s_k2, r_k2, s_v2, r_v2, s_ra, r_ra) = sems

    def copy(src, dst, send, recv, to):
        return pltpu.make_async_remote_copy(
            src_ref=src, dst_ref=dst, send_sem=send, recv_sem=recv, device_id=to, device_id_type=MESH
        )

    barrier = pltpu.get_barrier_semaphore()
    everyone = a_peers + x_peers + [y_peer, c_peer]
    for to in everyone:
        pl.semaphore_signal(barrier, inc=1, device_id=to, device_id_type=MESH)

    own_rows = pl.ds(pl.multiple_of(a * rows, rows), rows)
    kv[c, y, x, 0, own_rows, :] = k_ref[...]
    kv[c, y, x, 1, own_rows, :] = v_ref[...]
    fields = docs + 1
    own_info = a * fields
    pos_own = pos_ref[...]
    doc_own = doc_ref[...]
    info[c, y, x, own_info] = jnp.broadcast_to(pos_own[:, 0:1], (1, 128))
    for d in range(docs):
        tally = jnp.sum(jnp.where(doc_own == d, 1, 0), axis=1, keepdims=True)
        info[c, y, x, own_info + 1 + d] = jnp.broadcast_to(tally, (1, 128))

    pl.semaphore_wait(barrier, len(everyone))

    def a_kv(i):
        block = kv.at[c, y, x, :, own_rows, :]
        return copy(block, block, s_akv.at[i], r_akv.at[i], a_peers[i])

    def a_inf(i):
        block = info.at[c, y, x, pl.ds(own_info, fields)]
        return copy(block, block, s_ainf.at[i], r_ainf.at[i], a_peers[i])

    gather = [a_kv(i) for i in range(na - 1)] + [a_inf(i) for i in range(na - 1)]
    for one in gather:
        one.start()

    for h in range(heads):
        qs[h * rows : (h + 1) * rows, :] = q_ref[:, h * 128 : (h + 1) * 128]
        gs[h * rows : (h + 1) * rows, :] = g_ref[:, h * 128 : (h + 1) * 128]
    pos_q = jnp.concatenate([pos_own] * heads, axis=1)
    doc_q = jnp.concatenate([doc_own] * heads, axis=1)
    top[...] = jnp.full(top.shape, NEG_BIG, F32)
    den[...] = jnp.zeros(den.shape, F32)
    cross[...] = jnp.zeros(cross.shape, F32)
    dqt[...] = jnp.zeros(dqt.shape, F32)
    for one in gather:
        one.wait_recv()

    mine = kv.at[c, y, x]
    mine_info = info.at[c, y, x]
    direct = []
    for i in range(nx - 1):
        direct.append(copy(mine, mine, s_xkv.at[i], r_xkv.at[i], x_peers[i]))
        direct.append(copy(mine_info, mine_info, s_xinf.at[i], r_xinf.at[i], x_peers[i]))
    direct.append(copy(mine, mine, s_ykv, r_ykv, y_peer))
    direct.append(copy(mine_info, mine_info, s_yinf, r_yinf, y_peer))

    def place(step):
        return ((c + step // half) % CORES, (y + (step // nx) % SIDES) % SIDES, (x + step % nx) % nx)

    def to_core(step):
        _, yy, xx = place(step)
        return [
            copy(kv.at[c, yy, xx], kv.at[c, yy, xx], s_ckv.at[step], r_ckv.at[step], c_peer),
            copy(info.at[c, yy, xx], info.at[c, yy, xx], s_cinf.at[step], r_cinf.at[step], c_peer),
        ]

    forward = []
    for i in range(nx - 1):
        xx = (x + i + 1) % nx
        blk = kv.at[c, y, xx, 0]
        forward.append(copy(blk, blk, s_fk.at[i], r_fk.at[i], y_peer))
        blk = info.at[c, y, xx]
        forward.append(copy(blk, blk, s_finf.at[i], r_finf.at[i], y_peer))
        blk = kv.at[c, 1 - y, x, 1]
        forward.append(copy(blk, blk, s_fv.at[i], r_fv.at[i], x_peers[i]))

    for one in direct + to_core(0):
        one.start()

    row_ids = lax.broadcasted_iota(jnp.int32, (rows, lanes), 0)

    def widen(row):
        return jnp.concatenate([row] * (lanes // 128), axis=1) if lanes > 128 else row

    def look(step, carry):
        @pl.when(step == 1)
        def _():
            for one in direct:
                one.wait_recv()
            for one in forward:
                one.start()
            for s in [*range(1, nx), nx]:
                for one in to_core(s):
                    one.start()

        @pl.when(step == nx + 1)
        def _():
            for one in forward:
                one.wait_recv()
            for s in range(nx + 1, half):
                for one in to_core(s):
                    one.start()

        @pl.when(step >= half)
        def _():
            for one in to_core(step - half):
                one.wait_recv()

        cc, yy, xx = place(step)
        raw = dot(kv[cc, yy, xx, 0], qs[...], 1, 1)
        dprobs = dot(kv[cc, yy, xx, 1], gs[...], 1, 1)
        high = top[...]
        old = high
        for b in range(na):
            first = info[cc, yy, xx, b * fields]
            upper = pos_q - widen(first)
            lower = jnp.zeros((1, lanes), jnp.int32)
            for d in range(docs):
                lower = lower + jnp.where(doc_q > d, widen(info[cc, yy, xx, b * fields + 1 + d]), 0)
            seen = (row_ids >= lower) & (row_ids <= upper)
            part = jnp.where(seen, raw[b * rows : (b + 1) * rows, :] * scale, NEG_BIG)
            sbuf[step, b * rows : (b + 1) * rows, :] = part
            high = jnp.maximum(high, jnp.max(part, axis=0, keepdims=True))
        dpbuf[step] = dprobs
        fade = jnp.exp2(old - high)
        weights = jnp.exp2(sbuf[step] - high)
        top[...] = high
        den[...] = den[...] * fade + jnp.sum(weights, axis=0, keepdims=True)
        cross[...] = cross[...] * fade + jnp.sum(weights * dprobs, axis=0, keepdims=True)
        return carry

    lax.fori_loop(0, CORES * half, look, 0)

    log_total = top[...] + jnp.log2(den[...])
    row_dot = cross[...] / den[...]

    def grads(step):
        cc, yy, xx = place(step)
        probs = jnp.exp2(sbuf[step] - log_total)
        dscores = (probs * (dpbuf[step] - row_dot)).astype(BF16)
        dqt[...] += dot(kv[cc, yy, xx, 0], dscores, 0, 0)
        return dot(dscores, qs[...], 1, 0) * inv_root, dot(probs.astype(BF16), gs[...], 1, 0)

    def core_copy(slot):
        return copy(core_out.at[slot], core_in.at[slot], s_rc.at[slot], r_rc.at[slot], c_peer)

    def other_core(i, carry):
        slot = half - 1 - i
        dk, dv = grads(half + slot)
        core_out[slot, 0] = dk.astype(BF16)
        core_out[slot, 1] = dv.astype(BF16)
        core_copy(slot).start()
        return carry

    lax.fori_loop(0, half, other_core, 0)

    def k1_copy(r):
        return copy(yk_out.at[r], yk_in.at[r], s_k1.at[r], r_k1.at[r], y_peer)

    def v1_copy(side, i):
        at = side * (nx - 1) + i
        return copy(xv_out.at[at], xv_in.at[at], s_v1.at[at], r_v1.at[at], x_peers[i])

    def this_core(i, carry):
        slot = half - 1 - i
        side, r = slot // nx, slot % nx
        dk, dv = grads(slot)
        core_copy(slot).wait_recv()
        dk = dk + core_in[slot, 0].astype(F32)
        dv = dv + core_in[slot, 1].astype(F32)

        @pl.when(side == 1)
        def _():
            yk_out[r] = dk.astype(BF16)
            k1_copy(r).start()

        @pl.when(side == 0)
        def _():
            acck[r] = dk

        @pl.when(r == 0)
        def _():
            accv[side] = dv

        for j in range(nx - 1):
            @pl.when(r == j + 1)
            def _():
                xv_out[side * (nx - 1) + j] = dv.astype(BF16)
                v1_copy(side, j).start()

        return carry

    lax.fori_loop(0, half, this_core, 0)

    def k2_copy(i):
        return copy(xk_out.at[i], xk_in.at[i], s_k2.at[i], r_k2.at[i], x_peers[i])

    v2 = copy(yv_out, yv_in, s_v2, r_v2, y_peer)
    for i in range(nx - 1):
        k1_copy(i + 1).wait_recv()
        xk_out[i] = (acck[i + 1] + yk_in[i + 1].astype(F32)).astype(BF16)
        k2_copy(i).start()
    total = accv[1]
    for i in range(nx - 1):
        v1_copy(1, i).wait_recv()
        total = total + xv_in[(nx - 1) + i].astype(F32)
    yv_out[...] = total.astype(BF16)
    v2.start()

    dq = jnp.transpose(dqt[...]) * inv_root
    for h in range(heads):
        dq_ref[:, h * 128 : (h + 1) * 128] = dq[h * rows : (h + 1) * rows, :]

    k1_copy(0).wait_recv()
    total_k = acck[0] + yk_in[0].astype(F32)
    total_v = accv[0]
    for i in range(nx - 1):
        v1_copy(0, i).wait_recv()
        total_v = total_v + xv_in[i].astype(F32)
    for i in range(nx - 1):
        k2_copy(i).wait_recv()
        total_k = total_k + xk_in[i].astype(F32)
    v2.wait_recv()
    total_v = total_v + yv_in[...].astype(F32)
    a_own[0] = total_k
    a_own[1] = total_v
    a_out[0] = total_k.astype(BF16)
    a_out[1] = total_v.astype(BF16)

    def ra_copy(i):
        there = pl.ds(pl.multiple_of(((a + i + 1) % na) * rows, rows), rows)
        return copy(a_out.at[:, there, :], a_in.at[i], s_ra.at[i], r_ra.at[i], a_peers[i])

    for i in range(na - 1):
        ra_copy(i).start()
    out_k = a_own[0, own_rows, :]
    out_v = a_own[1, own_rows, :]
    for i in range(na - 1):
        ra_copy(i).wait_recv()
        out_k = out_k + a_in[i, 0].astype(F32)
        out_v = out_v + a_in[i, 1].astype(F32)
    dk_ref[...] = out_k
    dv_ref[...] = out_v

    for one in gather + direct + forward + [v2]:
        one.wait_send()
    for s in range(half):
        for one in to_core(s):
            one.wait_send()
        core_copy(s).wait_send()
    for r in range(nx):
        k1_copy(r).wait_send()
    for i in range(nx - 1):
        v1_copy(0, i).wait_send()
        v1_copy(1, i).wait_send()
        k2_copy(i).wait_send()
    for i in range(na - 1):
        ra_copy(i).wait_send()


def on_device(queries, key_vecs, value_vecs, out_grad, positions, documents):
    nx = lax.axis_size("head")
    na = lax.axis_size("ctx") // (CORES * SIDES)
    rows, width = queries.shape
    heads = width // 128
    seq = rows * nx * na * CORES * SIDES
    docs = max(2, seq // 1024)
    chunk, lanes, half = na * rows, heads * rows, SIDES * nx
    cfg = (nx, na, rows, heads, docs)
    dma = pltpu.SemaphoreType.DMA
    near = max(nx - 1, 1)
    far = max(na - 1, 1)
    pair = lambda shape: [dma(shape), dma(shape)]
    vmem = pltpu.VMEM
    scratch = [
        vmem((lanes, 128), BF16),
        vmem((lanes, 128), BF16),
        vmem((CORES, SIDES, nx, 2, chunk, 128), BF16),
        vmem((CORES, SIDES, nx, na * (docs + 1), 1, 128), jnp.int32),
        vmem((CORES * half, chunk, lanes), F32),
        vmem((CORES * half, chunk, lanes), F32),
        vmem((1, lanes), F32),
        vmem((1, lanes), F32),
        vmem((1, lanes), F32),
        vmem((128, lanes), F32),
        vmem((nx, chunk, 128), F32),
        vmem((SIDES, chunk, 128), F32),
        vmem((half, 2, chunk, 128), BF16),
        vmem((half, 2, chunk, 128), BF16),
        vmem((nx, chunk, 128), BF16),
        vmem((nx, chunk, 128), BF16),
        vmem((SIDES * near, chunk, 128), BF16),
        vmem((SIDES * near, chunk, 128), BF16),
        vmem((near, chunk, 128), BF16),
        vmem((near, chunk, 128), BF16),
        vmem((chunk, 128), BF16),
        vmem((chunk, 128), BF16),
        vmem((2, chunk, 128), BF16),
        vmem((far, 2, rows, 128), BF16),
        vmem((2, chunk, 128), F32),
        *pair((far,)), *pair((far,)),
        *pair((near,)), *pair((near,)),
        *pair(()), *pair(()),
        *pair((near,)), *pair((near,)), *pair((near,)),
        *pair((half,)), *pair((half,)),
        *pair((half,)),
        *pair((nx,)), *pair((SIDES * near,)), *pair((near,)), *pair(()),
        *pair((far,)),
    ]
    whole = pl.BlockSpec(memory_space=pltpu.VMEM)
    pairs = lanes * seq
    return pl.pallas_call(
        functools.partial(kernel, cfg),
        out_shape=(
            jax.ShapeDtypeStruct((rows, width), F32),
            jax.ShapeDtypeStruct((rows, 128), F32),
            jax.ShapeDtypeStruct((rows, 128), F32),
        ),
        in_specs=[whole] * 6,
        out_specs=(whole, whole, whole),
        scratch_shapes=scratch,
        compiler_params=pltpu.CompilerParams(
            collective_id=0, has_side_effects=True, vmem_limit_bytes=48 * 1024 * 1024
        ),
        cost_estimate=pl.CostEstimate(
            flops=10 * pairs * 128, bytes_accessed=rows * width * 8, transcendentals=2 * pairs
        ),
    )(queries, key_vecs, value_vecs, out_grad, positions.reshape(1, rows), documents.reshape(1, rows))


def solution(mesh):
    tokens = P(("head", "ctx"), None)
    ids = P(("head", "ctx"))
    return jax.shard_map(
        on_device,
        mesh=mesh,
        in_specs=(tokens, tokens, tokens, tokens, ids, ids),
        out_specs=(tokens, tokens, tokens),
        check_vma=False,
    )
```

```python
import functools
import math

import jax
import jax.numpy as jnp
from jax import lax
from jax.experimental import pallas as pl
from jax.experimental.pallas import tpu as pltpu
from jax.sharding import PartitionSpec as P

MESH = pl.DeviceIdType.MESH
NEG_BIG = -1e30
CORES = 2
SIDES = 2
F32 = jnp.float32
BF16 = jnp.bfloat16


def dot(lhs, rhs, lhs_dim, rhs_dim):
    return lax.dot_general(
        lhs, rhs, (((lhs_dim,), (rhs_dim,)), ((), ())), preferred_element_type=F32
    )


def xor(left, right, bits):
    total = 0
    for b in range(bits):
        total = total + ((left // 2**b + right // 2**b) % 2) * 2**b
    return total


def kernel(
    cfg,
    q_ref, k_ref, v_ref, g_ref, pos_ref, doc_ref,
    dq_ref, dk_ref, dv_ref,
    raw, qs, gs, kv, info, ids, sbuf, dpbuf, stats, dqt, dq_in, acck, accv,
    yk_out, yk_in, xv_out, xv_in, xk_out, xk_in, yv_out, yv_in, a_out, a_in, a_own,
    *sems,
):
    nx, na, rows, heads, docs, names = cfg
    sem = dict(zip(names, sems))
    lanes = heads * rows
    half = SIDES * nx
    x_bits, a_bits = (nx - 1).bit_length(), (na - 1).bit_length()
    inv_root = 1.0 / math.sqrt(128)
    scale = inv_root * math.log2(math.e)

    x = lax.axis_index("head")
    ctx = lax.axis_index("ctx")
    a, y, c = ctx // 4, (ctx // 2) % 2, ctx % 2

    def a_peer(r):
        return (x, xor(a, r, a_bits) * 4 + y * 2 + c)

    def x_peer(r):
        return (xor(x, r, x_bits), ctx)

    y_peer = (x, a * 4 + (1 - y) * 2 + c)
    c_peer = (x, a * 4 + y * 2 + 1 - c)

    def copy(src, dst, name, at, to):
        send, recv = sem["s_" + name], sem["r_" + name]
        return pltpu.make_async_remote_copy(
            src_ref=src, dst_ref=dst, send_sem=send.at[at], recv_sem=recv.at[at], device_id=to, device_id_type=MESH
        )

    barrier = pltpu.get_barrier_semaphore()
    everyone = [a_peer(r) for r in range(1, na)] + [x_peer(r) for r in range(1, nx)] + [y_peer, c_peer]
    for to in everyone:
        pl.semaphore_signal(barrier, inc=1, device_id=to, device_id_type=MESH)

    def rows_of(block):
        return pl.ds(pl.multiple_of(block * rows, rows), rows)

    own_rows = rows_of(a)
    own = [
        pltpu.make_async_copy(src, dst, sem["own"].at[i])
        for i, (src, dst) in enumerate([
            (pos_ref, ids.at[0]), (doc_ref, ids.at[1]),
            (k_ref, kv.at[y, x, 0, own_rows, :]), (v_ref, kv.at[y, x, 1, own_rows, :]),
            (q_ref, raw.at[0, c]), (g_ref, raw.at[1, c]),
        ])
    ]
    for one in own:
        one.start()

    pl.semaphore_wait(barrier, len(everyone))

    k_slot, v_slot = kv.at[y, x, 0, own_rows, :], kv.at[y, x, 1, own_rows, :]
    first = []
    for r in range(1, na):
        first.append(copy(k_ref, k_slot, "ak", r, a_peer(r)))
        first.append(copy(v_ref, v_slot, "av", r, a_peer(r)))
    first.append(copy(k_ref, k_slot, "y0k", 0, y_peer))
    first.append(copy(v_ref, v_slot, "y0v", 0, y_peer))
    for r in range(1, nx):
        first.append(copy(k_ref, k_slot, "x0k", r, x_peer(r)))
        first.append(copy(v_ref, v_slot, "x0v", r, x_peer(r)))
    for one in first:
        one.start()

    share = [copy(q_ref, raw.at[0, c], "qg", 0, c_peer), copy(g_ref, raw.at[1, c], "qg", 1, c_peer)]
    for one in share:
        one.start()

    fields = docs + 1
    own_info = a * fields
    own[0].wait()
    own[1].wait()
    pos_own = ids[0]
    doc_own = ids[1]
    info[y, x, own_info] = jnp.broadcast_to(pos_own[:, 0:1], (1, 128))
    for d in range(docs):
        tally = jnp.sum(jnp.where(doc_own == d, 1, 0), axis=1, keepdims=True)
        info[y, x, own_info + 1 + d] = jnp.broadcast_to(tally, (1, 128))
    info_slot = info.at[y, x, pl.ds(own_info, fields)]
    facts = [copy(info_slot, info_slot, "ainf", r, a_peer(r)) for r in range(1, na)]
    spare = 128 - 2 * rows
    pieces = [pos_own, doc_own] + ([jnp.zeros((1, spare), jnp.int32)] if spare else [])
    info_q = sem["info_q"]
    info_q[c] = jnp.concatenate(pieces, axis=1)
    facts.append(copy(info_q.at[c], info_q.at[c], "idq", 0, c_peer))
    for one in facts:
        one.start()

    def block_copies(step):
        block = kv.at[y, x, :, rows_of(xor(a, step, a_bits)), :]
        return [copy(block, block, "x", step * nx + r, x_peer(r)) for r in range(1, nx)] + [
            copy(block, block, "y", step, y_peer)
        ]

    def forwards(step):
        at = rows_of(xor(a, step, a_bits))
        found = []
        for r in range(1, nx):
            key_block = kv.at[y, xor(x, r, x_bits), 0, at, :]
            found.append(copy(key_block, key_block, "fk", step * nx + r, y_peer))
            value_block = kv.at[1 - y, x, 1, at, :]
            found.append(copy(value_block, value_block, "fv", step * nx + r, x_peer(r)))
        return found

    def a_arrived(step):
        block = kv.at[y, x, 0, own_rows, :]
        copy(block, block, "ak", step, a_peer(1)).wait_recv()
        copy(block, block, "av", step, a_peer(1)).wait_recv()

    def send_all(copies):
        for one in copies:
            one.start()

    def relay(step, carry):
        a_arrived(step)
        send_all(block_copies(step))

        @pl.when(step == 1)
        def _():
            for one in first[2 * (na - 1):]:
                one.wait_recv()

        @pl.when(step > 1)
        def _():
            for one in block_copies(step - 1):
                one.wait_recv()

        send_all(forwards(step - 1))
        return carry

    lax.fori_loop(1, na, relay, 0)

    for one in facts:
        one.wait_recv()
    mine_info = info.at[y, x]
    facts_xy = [copy(mine_info, mine_info, "xinf", r, x_peer(r)) for r in range(1, nx)]
    facts_xy.append(copy(mine_info, mine_info, "yinf", 0, y_peer))
    send_all(facts_xy)

    for one in own[2:]:
        one.wait()
    for one in share:
        one.wait_recv()
    for k in range(CORES):
        for h in range(heads):
            at = k * lanes + h * rows
            qs[at : at + rows, :] = raw[0, k, :, h * 128 : (h + 1) * 128]
            gs[at : at + rows, :] = raw[1, k, :, h * 128 : (h + 1) * 128]
    both = [info_q[k] for k in range(CORES)]
    pos_q = jnp.concatenate([one[:, :rows] for one in both for _ in range(heads)], axis=1)
    doc_q = jnp.concatenate([one[:, rows : 2 * rows] for one in both for _ in range(heads)], axis=1)
    wide = CORES * lanes
    stats[0] = jnp.full((1, wide), NEG_BIG, F32)
    stats[1] = jnp.zeros((1, wide), F32)
    stats[2] = jnp.zeros((1, wide), F32)
    dqt[...] = jnp.zeros(dqt.shape, F32)

    def place(step):
        return ((y + step // nx) % SIDES, xor(x, step % nx, x_bits))

    facts_fwd = []
    for r in range(1, nx):
        blk = info.at[y, xor(x, r, x_bits)]
        facts_fwd.append(copy(blk, blk, "finf", r, y_peer))

    row_ids = lax.broadcasted_iota(jnp.int32, (rows, wide), 0)

    def widen(row):
        return jnp.concatenate([row] * (wide // 128), axis=1)

    def look(step, carry):
        @pl.when(step == 1)
        def _():
            for one in block_copies(na - 1):
                one.wait_recv()
            send_all(forwards(na - 1))
            for one in facts_xy:
                one.wait_recv()
            send_all(facts_fwd)

        @pl.when(step == nx + 1)
        def _():
            for one in facts_fwd:
                one.wait_recv()
            for s in range(na):
                for one in forwards(s):
                    one.wait_recv()

        yy, xx = place(step)
        scores = dot(kv[yy, xx, 0], qs[...], 1, 1)
        dprobs = dot(kv[yy, xx, 1], gs[...], 1, 1)
        old = stats[0]
        high = old
        for b in range(na):
            upper = pos_q - widen(info[yy, xx, b * fields])
            lower = jnp.zeros((1, wide), jnp.int32)
            for d in range(docs):
                lower = lower + jnp.where(doc_q > d, widen(info[yy, xx, b * fields + 1 + d]), 0)
            seen = (row_ids >= lower) & (row_ids <= upper)
            part = jnp.where(seen, scores[b * rows : (b + 1) * rows, :] * scale, NEG_BIG)
            sbuf[step, b * rows : (b + 1) * rows, :] = part
            high = jnp.maximum(high, jnp.max(part, axis=0, keepdims=True))
        dpbuf[step] = dprobs
        fade = jnp.exp2(old - high)
        weights = jnp.exp2(sbuf[step] - high)
        stats[0] = high
        stats[1] = stats[1] * fade + jnp.sum(weights, axis=0, keepdims=True)
        stats[2] = stats[2] * fade + jnp.sum(weights * dprobs, axis=0, keepdims=True)
        return carry

    lax.fori_loop(0, half, look, 0)

    stats_in = sem["stats_in"]
    swap = copy(stats, stats_in, "stat", 0, c_peer)
    swap.start()
    swap.wait_recv()
    high = jnp.maximum(stats[0], stats_in[0])
    here, there = jnp.exp2(stats[0] - high), jnp.exp2(stats_in[0] - high)
    denom = stats[1] * here + stats_in[1] * there
    log_total = high + jnp.log2(denom)
    row_dot = (stats[2] * here + stats_in[2] * there) / denom

    def k1_copy(r):
        return copy(yk_out.at[r], yk_in.at[r], "k1", r, y_peer)

    def v1_copy(side, r):
        at = side * nx + r
        return copy(xv_out.at[at], xv_in.at[at], "v1", at, x_peer(r))

    def grads(i, carry):
        step = half - 1 - i
        side, r = step // nx, step % nx
        yy, xx = place(step)
        probs = jnp.exp2(sbuf[step] - log_total)
        dscores = (probs * (dpbuf[step] - row_dot)).astype(BF16)
        dk = dot(dscores, qs[...], 1, 0) * inv_root
        dv = dot(probs.astype(BF16), gs[...], 1, 0)

        @pl.when(side == 1)
        def _():
            yk_out[r] = dk.astype(BF16)
            k1_copy(r).start()

        @pl.when(side == 0)
        def _():
            acck[r] = dk

        @pl.when(r == 0)
        def _():
            accv[side] = dv

        @pl.when(r > 0)
        def _():
            xv_out[side * nx + r] = dv.astype(BF16)
            v1_copy(side, r).start()

        part = dot(kv[yy, xx, 0], dscores, 0, 0)
        for k in range(CORES):
            dqt[k] += part[:, k * lanes : (k + 1) * lanes]
        return carry

    lax.fori_loop(0, half, grads, 0)

    def k2_copy(r):
        return copy(xk_out.at[r], xk_in.at[r], "k2", r, x_peer(r))

    v2 = copy(yv_out, yv_in, "v2", 0, y_peer)
    swap_dq = copy(dqt.at[1 - c], dq_in, "dq", 0, c_peer)
    for r in range(1, nx):
        k1_copy(r).wait_recv()
        xk_out[r] = (acck[r] + yk_in[r].astype(F32)).astype(BF16)
        k2_copy(r).start()
    total = accv[1]
    for r in range(1, nx):
        v1_copy(1, r).wait_recv()
        total = total + xv_in[nx + r].astype(F32)
    yv_out[...] = total.astype(BF16)
    v2.start()
    swap_dq.start()

    k1_copy(0).wait_recv()
    total_k = acck[0] + yk_in[0].astype(F32)
    a_own[0] = total_k
    total_v = accv[0]
    for r in range(1, nx):
        v1_copy(0, r).wait_recv()
        total_v = total_v + xv_in[r].astype(F32)
    a_own[1] = total_v

    dq_own = sem["dq_own"]
    swap_dq.wait_recv()
    dq = jnp.transpose(dqt[c] + dq_in[...]) * inv_root
    for h in range(heads):
        dq_own[:, h * 128 : (h + 1) * 128] = dq[h * rows : (h + 1) * rows, :]
    results = [
        pltpu.make_async_copy(src, dst, sem["out"].at[i])
        for i, (src, dst) in enumerate([(dq_own, dq_ref), (sem["dk_own"], dk_ref), (sem["dv_own"], dv_ref)])
    ]
    results[0].start()

    def ra_copy(which, r):
        at = which * na + r
        src = a_out.at[which, rows_of(xor(a, r, a_bits)), :]
        return copy(src, a_in.at[at], "ra", at, a_peer(r))

    total_k = a_own[0]
    for r in range(1, nx):
        k2_copy(r).wait_recv()
        total_k = total_k + xk_in[r].astype(F32)
    a_out[0] = total_k.astype(BF16)
    a_own[0] = total_k
    for r in range(1, na):
        ra_copy(0, r).start()
    v2.wait_recv()
    total_v = a_own[1] + yv_in[...].astype(F32)
    a_out[1] = total_v.astype(BF16)
    a_own[1] = total_v
    for r in range(1, na):
        ra_copy(1, r).start()

    for one in first + share + facts + facts_xy + facts_fwd + [swap, v2, swap_dq]:
        one.wait_send()

    def sent(step, carry):
        @pl.when(step > 0)
        def _():
            for one in block_copies(step):
                one.wait_send()

        for one in forwards(step):
            one.wait_send()
        return carry

    lax.fori_loop(0, na, sent, 0)
    for r in range(nx):
        k1_copy(r).wait_send()
    for r in range(1, nx):
        v1_copy(0, r).wait_send()
        v1_copy(1, r).wait_send()
        k2_copy(r).wait_send()

    for which, out in ((0, sem["dk_own"]), (1, sem["dv_own"])):
        done = a_own[which, own_rows, :]
        for r in range(1, na):
            ra_copy(which, r).wait_recv()
            done = done + a_in[which * na + r].astype(F32)
        out[...] = done
        results[1 + which].start()
    for which in range(2):
        for r in range(1, na):
            ra_copy(which, r).wait_send()
    for one in results:
        one.wait()


def hand_over(*refs):
    count = (len(refs) - 1) // 2
    moves = [pltpu.make_async_copy(refs[i], refs[count + i], refs[-1].at[i]) for i in range(count)]
    for one in moves:
        one.start()
    for one in moves:
        one.wait()


def on_device(queries, key_vecs, value_vecs, out_grad, positions, documents):
    nx = lax.axis_size("head")
    na = lax.axis_size("ctx") // (CORES * SIDES)
    rows, width = queries.shape
    heads = width // 128
    seq = rows * nx * na * CORES * SIDES
    docs = max(2, seq // 1024)
    chunk, lanes, half = na * rows, heads * rows, SIDES * nx
    wide = CORES * lanes
    dma = pltpu.SemaphoreType.DMA
    vmem = pltpu.VMEM
    copies = {
        "ak": na, "av": na, "ainf": na, "idq": 1, "y0k": 1, "y0v": 1, "x0k": nx, "x0v": nx, "qg": 2,
        "x": na * nx, "y": na, "fk": na * nx, "fv": na * nx, "xinf": nx, "yinf": 1, "finf": nx, "stat": 1,
        "k1": nx, "v1": SIDES * nx, "k2": nx, "v2": 1, "dq": 1, "ra": 2 * na,
    }
    names, tail = [], []
    for name, count in copies.items():
        names += ["s_" + name, "r_" + name]
        tail += [dma((count,)), dma((count,))]
    names += ["own", "out", "info_q", "stats_in", "dq_own", "dk_own", "dv_own"]
    tail += [dma((6,)), dma((3,)), vmem((CORES, 1, 128), jnp.int32), vmem((3, 1, wide), F32)]
    tail += [vmem((rows, width), F32), vmem((rows, 128), F32), vmem((rows, 128), F32)]
    scratch = [
        vmem((2, CORES, rows, width), BF16),
        vmem((wide, 128), BF16),
        vmem((wide, 128), BF16),
        vmem((SIDES, nx, 2, chunk, 128), BF16),
        vmem((SIDES, nx, na * (docs + 1), 1, 128), jnp.int32),
        vmem((2, 1, rows), jnp.int32),
        vmem((half, chunk, wide), F32),
        vmem((half, chunk, wide), F32),
        vmem((3, 1, wide), F32),
        vmem((CORES, 128, lanes), F32),
        vmem((128, lanes), F32),
        vmem((nx, chunk, 128), F32),
        vmem((SIDES, chunk, 128), F32),
        vmem((nx, chunk, 128), BF16),
        vmem((nx, chunk, 128), BF16),
        vmem((SIDES * nx, chunk, 128), BF16),
        vmem((SIDES * nx, chunk, 128), BF16),
        vmem((nx, chunk, 128), BF16),
        vmem((nx, chunk, 128), BF16),
        vmem((chunk, 128), BF16),
        vmem((chunk, 128), BF16),
        vmem((2, chunk, 128), BF16),
        vmem((2 * na, rows, 128), BF16),
        vmem((2, chunk, 128), F32),
    ] + tail
    cfg = (nx, na, rows, heads, docs, names)
    far = pl.BlockSpec(memory_space=pltpu.HBM)
    pairs = lanes * seq
    shapes = (
        jax.ShapeDtypeStruct((rows, width), F32),
        jax.ShapeDtypeStruct((rows, 128), F32),
        jax.ShapeDtypeStruct((rows, 128), F32),
    )
    found = pl.pallas_call(
        functools.partial(kernel, cfg),
        out_shape=shapes,
        in_specs=[far] * 6,
        out_specs=(far, far, far),
        scratch_shapes=scratch,
        compiler_params=pltpu.CompilerParams(
            collective_id=0, has_side_effects=True, vmem_limit_bytes=64 * 1024 * 1024
        ),
        cost_estimate=pl.CostEstimate(
            flops=10 * pairs * 128, bytes_accessed=rows * width * 8, transcendentals=2 * pairs
        ),
    )(queries, key_vecs, value_vecs, out_grad, positions.reshape(1, rows), documents.reshape(1, rows))
    return pl.pallas_call(
        hand_over,
        out_shape=shapes,
        in_specs=[far] * 3,
        out_specs=(far, far, far),
        scratch_shapes=[dma((3,))],
        compiler_params=pltpu.CompilerParams(vmem_limit_bytes=64 * 1024 * 1024),
    )(*found)


def solution(mesh):
    tokens = P(("head", "ctx"), None)
    ids = P(("head", "ctx"))
    return jax.shard_map(
        on_device,
        mesh=mesh,
        in_specs=(tokens, tokens, tokens, tokens, ids, ids),
        out_specs=(tokens, tokens, tokens),
        check_vma=False,
    )
```

```python
import functools
import math

import jax
import jax.numpy as jnp
from jax import lax
from jax.experimental import pallas as pl
from jax.experimental.pallas import tpu as pltpu
from jax.sharding import PartitionSpec as P

MESH = pl.DeviceIdType.MESH
NEG_BIG = -1e30
CORES = 2
LAG = 2
SIDES = 2
F32 = jnp.float32
BF16 = jnp.bfloat16


def dot(lhs, rhs, lhs_dim, rhs_dim):
    return lax.dot_general(
        lhs, rhs, (((lhs_dim,), (rhs_dim,)), ((), ())), preferred_element_type=F32
    )


def xor(left, right, bits):
    total = 0
    for b in range(bits):
        total = total + ((left // 2**b + right // 2**b) % 2) * 2**b
    return total


def kernel(
    cfg,
    q_ref, k_ref, v_ref, g_ref, pos_ref, doc_ref,
    dq_ref, dk_ref, dv_ref,
    raw, qs, gs, kv, info, ids, sbuf, dpbuf, stats, dqt, dq_in, acck, accv,
    k_out, yk_in, v_out, xv_in, xk_out, xk_in, yv_out, yv_in, a_out, a_in, a_own,
    *sems,
):
    nx, na, rows, heads, docs, names = cfg
    sem = dict(zip(names, sems))
    lanes = heads * rows
    group = SIDES * nx
    x_bits, a_bits = (nx - 1).bit_length(), (na - 1).bit_length()
    inv_root = 1.0 / math.sqrt(128)
    scale = inv_root * math.log2(math.e)

    x = lax.axis_index("head")
    ctx = lax.axis_index("ctx")
    a, y, c = ctx // 4, (ctx // 2) % 2, ctx % 2

    def a_peer(r):
        return (x, xor(a, r, a_bits) * 4 + y * 2 + c)

    def x_peer(r):
        return (xor(x, r, x_bits), ctx)

    y_peer = (x, a * 4 + (1 - y) * 2 + c)
    c_peer = (x, a * 4 + y * 2 + 1 - c)

    def copy(src, dst, name, at, to):
        send, recv = sem["s_" + name], sem["r_" + name]
        return pltpu.make_async_remote_copy(
            src_ref=src, dst_ref=dst, send_sem=send.at[at], recv_sem=recv.at[at], device_id=to, device_id_type=MESH
        )

    barrier = pltpu.get_barrier_semaphore()
    everyone = [a_peer(r) for r in range(1, na)] + [x_peer(r) for r in range(1, nx)] + [y_peer, c_peer]
    for to in everyone:
        pl.semaphore_signal(barrier, inc=1, device_id=to, device_id_type=MESH)

    k_slot, v_slot = kv.at[a, 0, y, x], kv.at[a, 1, y, x]
    own = [
        pltpu.make_async_copy(src, dst, sem["own"].at[i])
        for i, (src, dst) in enumerate([
            (pos_ref, ids.at[0]), (doc_ref, ids.at[1]),
            (k_ref, k_slot), (v_ref, v_slot),
            (q_ref, raw.at[0, c]), (g_ref, raw.at[1, c]),
        ])
    ]
    for one in own:
        one.start()

    pl.semaphore_wait(barrier, len(everyone))

    first = []
    for r in range(1, na):
        first.append(copy(k_ref, k_slot, "ak", r, a_peer(r)))
        first.append(copy(v_ref, v_slot, "av", r, a_peer(r)))
    first.append(copy(k_ref, k_slot, "y0k", 0, y_peer))
    first.append(copy(v_ref, v_slot, "y0v", 0, y_peer))
    for r in range(1, nx):
        first.append(copy(k_ref, k_slot, "x0k", r, x_peer(r)))
        first.append(copy(v_ref, v_slot, "x0v", r, x_peer(r)))
    for one in first:
        one.start()

    share = [copy(q_ref, raw.at[0, c], "qg", 0, c_peer), copy(g_ref, raw.at[1, c], "qg", 1, c_peer)]
    for one in share:
        one.start()

    fields = docs + 1
    own[0].wait()
    own[1].wait()
    pos_own = ids[0]
    doc_own = ids[1]
    info[a, y, x, 0] = jnp.broadcast_to(pos_own[:, 0:1], (1, 128))
    for d in range(docs):
        tally = jnp.sum(jnp.where(doc_own == d, 1, 0), axis=1, keepdims=True)
        info[a, y, x, 1 + d] = jnp.broadcast_to(tally, (1, 128))
    info_slot = info.at[a, y, x]
    facts_x = [copy(info_slot, info_slot, "xinf", r, x_peer(r)) for r in range(1, nx)]
    facts = facts_x + [copy(info_slot, info_slot, "yinf", 0, y_peer)]
    spare = 128 - 2 * rows
    pieces = [pos_own, doc_own] + ([jnp.zeros((1, spare), jnp.int32)] if spare else [])
    info_q = sem["info_q"]
    info_q[c] = jnp.concatenate(pieces, axis=1)
    id_share = copy(info_q.at[c], info_q.at[c], "idq", 0, c_peer)
    for one in facts + [id_share]:
        one.start()

    def block_copies(step):
        block = kv.at[xor(a, step, a_bits), :, y, x]
        return [copy(block, block, "x", step * nx + r, x_peer(r)) for r in range(1, nx)] + [
            copy(block, block, "y", step, y_peer)
        ]

    def forwards(step):
        at = xor(a, step, a_bits)
        found = []
        for r in range(1, nx):
            key_block = kv.at[at, 0, y, xor(x, r, x_bits)]
            found.append(copy(key_block, key_block, "fk", step * nx + r, y_peer))
            value_block = kv.at[at, 1, 1 - y, x]
            found.append(copy(value_block, value_block, "fv", step * nx + r, x_peer(r)))
        return found

    def a_arrived(step):
        block = k_slot
        copy(block, block, "ak", step, a_peer(1)).wait_recv()
        copy(block, block, "av", step, a_peer(1)).wait_recv()

    def send_all(copies):
        for one in copies:
            one.start()

    def relay(step, carry):
        a_arrived(step)
        send_all(block_copies(step))

        @pl.when(step == 1)
        def _():
            for one in first[2 * (na - 1):]:
                one.wait_recv()

        @pl.when(step > 1)
        def _():
            for one in block_copies(step - 1):
                one.wait_recv()

        send_all(forwards(step - 1))
        return carry

    facts_fwd = []
    for r in range(1, nx):
        blk = info.at[a, y, xor(x, r, x_bits)]
        facts_fwd.append(copy(blk, blk, "finf", r, y_peer))
    facts_a = [copy(info.at[a], info.at[a], "ainf", r, a_peer(r)) for r in range(1, na)]
    for one in facts_x:
        one.wait_recv()
    send_all(facts_fwd)
    for one in facts[nx - 1:] + facts_fwd:
        one.wait_recv()
    send_all(facts_a)

    lax.fori_loop(1, na, relay, 0)

    for one in own[2:]:
        one.wait()
    for one in share + [id_share]:
        one.wait_recv()
    for k in range(CORES):
        for h in range(heads):
            at = k * lanes + h * rows
            qs[at : at + rows, :] = raw[0, k, :, h * 128 : (h + 1) * 128]
            gs[at : at + rows, :] = raw[1, k, :, h * 128 : (h + 1) * 128]
    both = [info_q[k] for k in range(CORES)]
    pos_q = jnp.concatenate([one[:, :rows] for one in both for _ in range(heads)], axis=1)
    doc_q = jnp.concatenate([one[:, rows : 2 * rows] for one in both for _ in range(heads)], axis=1)
    wide = CORES * lanes
    stats[0] = jnp.full((1, wide), NEG_BIG, F32)
    stats[1] = jnp.zeros((1, wide), F32)
    stats[2] = jnp.zeros((1, wide), F32)
    dqt[...] = jnp.zeros(dqt.shape, F32)
    for one in facts_a:
        one.wait_recv()

    row_ids = lax.broadcasted_iota(jnp.int32, (rows, wide), 0)

    def widen(row):
        return jnp.concatenate([row] * (wide // 128), axis=1)

    def chunk_of(step, which):
        return kv[xor(a, step, a_bits), which].reshape(group * rows, 128)

    def look(step, carry):
        @pl.when(step == 1)
        def _():
            for one in block_copies(na - 1):
                one.wait_recv()
            send_all(forwards(na - 1))

        for one in forwards(step):
            one.wait_recv()

        scores = dot(chunk_of(step, 0), qs[...], 1, 1)
        dprobs = dot(chunk_of(step, 1), gs[...], 1, 1)
        old = stats[0]
        high = old
        at = xor(a, step, a_bits)
        for b in range(group):
            row = lambda f: widen(info[at, b // nx, b % nx, f])
            upper = pos_q - row(0)
            lower = jnp.zeros((1, wide), jnp.int32)
            for d in range(docs):
                lower = lower + jnp.where(doc_q > d, row(1 + d), 0)
            seen = (row_ids >= lower) & (row_ids <= upper)
            part = jnp.where(seen, scores[b * rows : (b + 1) * rows, :] * scale, NEG_BIG)
            sbuf[step, b * rows : (b + 1) * rows, :] = part
            high = jnp.maximum(high, jnp.max(part, axis=0, keepdims=True))
        dpbuf[step] = dprobs
        fade = jnp.exp2(old - high)
        weights = jnp.exp2(sbuf[step] - high)
        stats[0] = high
        stats[1] = stats[1] * fade + jnp.sum(weights, axis=0, keepdims=True)
        stats[2] = stats[2] * fade + jnp.sum(weights * dprobs, axis=0, keepdims=True)
        return carry

    lax.fori_loop(0, na, look, 0)

    stats_in = sem["stats_in"]
    swap = copy(stats, stats_in, "stat", 0, c_peer)
    swap.start()
    swap.wait_recv()
    high = jnp.maximum(stats[0], stats_in[0])
    here, there = jnp.exp2(stats[0] - high), jnp.exp2(stats_in[0] - high)
    denom = stats[1] * here + stats_in[1] * there
    log_total = high + jnp.log2(denom)
    row_dot = (stats[2] * here + stats_in[2] * there) / denom

    def k1_copy(step):
        return copy(k_out.at[step, 1 - y], yk_in.at[step], "k1", step, y_peer)

    def v1_copy(step, r):
        at = step * nx + r
        return copy(v_out.at[step, :, xor(x, r, x_bits)], xv_in.at[at], "v1", at, x_peer(r))

    def k2_copy(step, r):
        at = step * nx + r
        return copy(xk_out.at[at], xk_in.at[at], "k2", at, x_peer(r))

    def v2_copy(step):
        return copy(yv_out.at[step], yv_in.at[step], "v2", step, y_peer)

    def ra_copy(step):
        return copy(a_out.at[step], a_in.at[step], "ra", step, a_peer(step))

    def grads(step):
        probs = jnp.exp2(sbuf[step] - log_total)
        dscores = (probs * (dpbuf[step] - row_dot)).astype(BF16)
        dk = dot(dscores, qs[...], 1, 0) * inv_root
        dv = dot(probs.astype(BF16), gs[...], 1, 0)
        dk = dk.reshape(SIDES, nx, rows, 128)
        dv = dv.reshape(SIDES, nx, rows, 128)
        k_out[step] = dk.astype(BF16)
        v_out[step] = dv.astype(BF16)
        k1_copy(step).start()
        for r in range(1, nx):
            v1_copy(step, r).start()
        acck[step] = dk
        accv[step] = dv
        part = dot(chunk_of(step, 0), dscores, 0, 0)
        for k in range(CORES):
            dqt[k] += part[:, k * lanes : (k + 1) * lanes]

    def second(step):
        k1_copy(step).wait_recv()
        for r in range(1, nx):
            xx = xor(x, r, x_bits)
            both_y = acck[step, y, xx] + yk_in[step, xx].astype(F32)
            xk_out[step * nx + r] = both_y.astype(BF16)
            k2_copy(step, r).start()
        other, here_v = accv[step, 1 - y, x], accv[step, y, x]
        for r in range(1, nx):
            v1_copy(step, r).wait_recv()
            other = other + xv_in[step * nx + r, 1 - y].astype(F32)
            here_v = here_v + xv_in[step * nx + r, y].astype(F32)
        yv_out[step] = other.astype(BF16)
        v2_copy(step).start()
        a_own[step, 0] = acck[step, y, x] + yk_in[step, x].astype(F32)
        a_own[step, 1] = here_v

    def third(step):
        total = a_own[step, 0]
        for r in range(1, nx):
            k2_copy(step, r).wait_recv()
            total = total + xk_in[step * nx + r].astype(F32)
        v2_copy(step).wait_recv()
        total_v = a_own[step, 1] + yv_in[step].astype(F32)
        a_own[step, 0] = total
        a_own[step, 1] = total_v

        @pl.when(step > 0)
        def _():
            a_out[step, 0] = total.astype(BF16)
            a_out[step, 1] = total_v.astype(BF16)
            ra_copy(step).start()

    def turn(i, carry):
        grads(na - 1 - i)

        @pl.when(i >= LAG)
        def _():
            second(na - 1 - i + LAG)

        @pl.when(i >= 2 * LAG)
        def _():
            third(na - 1 - i + 2 * LAG)

        return carry

    lax.fori_loop(0, na, turn, 0)
    dq_own = sem["dq_own"]
    swap_dq = copy(dqt.at[1 - c], dq_in, "dq", 0, c_peer)
    swap_dq.start()

    for step in range(min(LAG, na) - 1, -1, -1):
        second(step)
        if step + LAG < na:
            third(step + LAG)
    swap_dq.wait_recv()
    dq = jnp.transpose(dqt[c] + dq_in[...]) * inv_root
    for h in range(heads):
        dq_own[:, h * 128 : (h + 1) * 128] = dq[h * rows : (h + 1) * rows, :]
    results = [
        pltpu.make_async_copy(src, dst, sem["out"].at[i])
        for i, (src, dst) in enumerate([(dq_own, dq_ref), (sem["dk_own"], dk_ref), (sem["dv_own"], dv_ref)])
    ]
    results[0].start()

    for step in range(min(LAG, na) - 1, -1, -1):
        third(step)

    for one in first + share + [id_share] + facts + facts_fwd + facts_a + [swap, swap_dq]:
        one.wait_send()

    def sent(step, carry):
        @pl.when(step > 0)
        def _():
            for one in block_copies(step):
                one.wait_send()
            ra_copy(step).wait_send()

        for one in forwards(step):
            one.wait_send()
        k1_copy(step).wait_send()
        v2_copy(step).wait_send()
        for r in range(1, nx):
            v1_copy(step, r).wait_send()
            k2_copy(step, r).wait_send()
        return carry

    lax.fori_loop(0, na, sent, 0)

    def collect(step, carry):
        ra_copy(step).wait_recv()
        return carry + a_in[step].astype(F32)

    done = lax.fori_loop(1, na, collect, a_own[0])
    sem["dk_own"][...] = done[0]
    sem["dv_own"][...] = done[1]
    results[1].start()
    results[2].start()
    for one in results:
        one.wait()


def hand_over(*refs):
    count = (len(refs) - 1) // 2
    moves = [pltpu.make_async_copy(refs[i], refs[count + i], refs[-1].at[i]) for i in range(count)]
    for one in moves:
        one.start()
    for one in moves:
        one.wait()


def on_device(queries, key_vecs, value_vecs, out_grad, positions, documents):
    nx = lax.axis_size("head")
    na = lax.axis_size("ctx") // (CORES * SIDES)
    rows, width = queries.shape
    heads = width // 128
    seq = rows * nx * na * CORES * SIDES
    docs = max(2, seq // 1024)
    lanes, group = heads * rows, SIDES * nx
    chunk = group * rows
    wide = CORES * lanes
    dma = pltpu.SemaphoreType.DMA
    vmem = pltpu.VMEM
    copies = {
        "ak": na, "av": na, "ainf": na, "idq": 1, "y0k": 1, "y0v": 1, "x0k": nx, "x0v": nx, "qg": 2,
        "x": na * nx, "y": na, "fk": na * nx, "fv": na * nx, "xinf": nx, "yinf": 1, "finf": nx, "stat": 1,
        "k1": na, "v1": na * nx, "k2": na * nx, "v2": na, "dq": 1, "ra": na,
    }
    names, tail = [], []
    for name, count in copies.items():
        names += ["s_" + name, "r_" + name]
        tail += [dma((count,)), dma((count,))]
    names += ["own", "out", "info_q", "stats_in", "dq_own", "dk_own", "dv_own"]
    tail += [dma((6,)), dma((3,)), vmem((CORES, 1, 128), jnp.int32), vmem((3, 1, wide), F32)]
    tail += [vmem((rows, width), F32), vmem((rows, 128), F32), vmem((rows, 128), F32)]
    scratch = [
        vmem((2, CORES, rows, width), BF16),
        vmem((wide, 128), BF16),
        vmem((wide, 128), BF16),
        vmem((na, 2, SIDES, nx, rows, 128), BF16),
        vmem((na, SIDES, nx, docs + 1, 1, 128), jnp.int32),
        vmem((2, 1, rows), jnp.int32),
        vmem((na, chunk, wide), F32),
        vmem((na, chunk, wide), F32),
        vmem((3, 1, wide), F32),
        vmem((CORES, 128, lanes), F32),
        vmem((128, lanes), F32),
        vmem((na, SIDES, nx, rows, 128), F32),
        vmem((na, SIDES, nx, rows, 128), F32),
        vmem((na, SIDES, nx, rows, 128), BF16),
        vmem((na, nx, rows, 128), BF16),
        vmem((na, SIDES, nx, rows, 128), BF16),
        vmem((na * nx, SIDES, rows, 128), BF16),
        vmem((na * nx, rows, 128), BF16),
        vmem((na * nx, rows, 128), BF16),
        vmem((na, rows, 128), BF16),
        vmem((na, rows, 128), BF16),
        vmem((na, 2, rows, 128), BF16),
        vmem((na, 2, rows, 128), BF16),
        vmem((na, 2, rows, 128), F32),
    ] + tail
    cfg = (nx, na, rows, heads, docs, names)
    far = pl.BlockSpec(memory_space=pltpu.HBM)
    pairs = lanes * seq
    shapes = (
        jax.ShapeDtypeStruct((rows, width), F32),
        jax.ShapeDtypeStruct((rows, 128), F32),
        jax.ShapeDtypeStruct((rows, 128), F32),
    )
    found = pl.pallas_call(
        functools.partial(kernel, cfg),
        out_shape=shapes,
        in_specs=[far] * 6,
        out_specs=(far, far, far),
        scratch_shapes=scratch,
        compiler_params=pltpu.CompilerParams(
            collective_id=0, has_side_effects=True, vmem_limit_bytes=64 * 1024 * 1024
        ),
        cost_estimate=pl.CostEstimate(
            flops=10 * pairs * 128, bytes_accessed=rows * width * 8, transcendentals=2 * pairs
        ),
    )(queries, key_vecs, value_vecs, out_grad, positions.reshape(1, rows), documents.reshape(1, rows))
    return pl.pallas_call(
        hand_over,
        out_shape=shapes,
        in_specs=[pl.BlockSpec(memory_space=pltpu.VMEM)] * 3,
        out_specs=(far, far, far),
        scratch_shapes=[dma((3,))],
        compiler_params=pltpu.CompilerParams(vmem_limit_bytes=64 * 1024 * 1024),
    )(*found)


def solution(mesh):
    tokens = P(("head", "ctx"), None)
    ids = P(("head", "ctx"))
    return jax.shard_map(
        on_device,
        mesh=mesh,
        in_specs=(tokens, tokens, tokens, tokens, ids, ids),
        out_specs=(tokens, tokens, tokens),
        check_vma=False,
    )
```

```python
import functools
import math

import jax
import jax.numpy as jnp
from jax import lax
from jax.experimental import pallas as pl
from jax.experimental.pallas import tpu as pltpu
from jax.sharding import PartitionSpec as P

MESH = pl.DeviceIdType.MESH
NEG_BIG = -1e30
CORES = 2
LAG = 2
SIDES = 2
F32 = jnp.float32
BF16 = jnp.bfloat16


def dot(lhs, rhs, lhs_dim, rhs_dim):
    return lax.dot_general(
        lhs, rhs, (((lhs_dim,), (rhs_dim,)), ((), ())), preferred_element_type=F32
    )


def xor(left, right, bits):
    total = 0
    for b in range(bits):
        total = total + ((left // 2**b + right // 2**b) % 2) * 2**b
    return total


def kernel(
    cfg,
    q_ref, k_ref, v_ref, g_ref, pos_ref, doc_ref,
    dq_ref, dk_ref, dv_ref,
    raw, qs, gs, qt, gt, kv, info, ids, sbuf, dpbuf, stats, dqt, dq_in, acc, g_out, g_in, a_out, a_in, a_own,
    *sems,
):
    nx, na, rows, heads, docs, names = cfg
    sem = dict(zip(names, sems))
    lanes = heads * rows
    group = SIDES * nx
    x_bits, a_bits = (nx - 1).bit_length(), (na - 1).bit_length()
    inv_root = 1.0 / math.sqrt(128)
    scale = inv_root * math.log2(math.e)

    x = lax.axis_index("head")
    ctx = lax.axis_index("ctx")
    a, y, c = ctx // 4, (ctx // 2) % 2, ctx % 2

    def a_peer(r):
        return (x, xor(a, r, a_bits) * 4 + y * 2 + c)

    def group_place(r):
        return ((y + r // nx) % SIDES, xor(x, r % nx, x_bits))

    def group_peer(r):
        yy, xx = group_place(r)
        return (xx, a * 4 + yy * 2 + c)

    c_peer = (x, a * 4 + y * 2 + 1 - c)

    def copy(src, dst, name, at, to):
        send, recv = sem["s_" + name], sem["r_" + name]
        return pltpu.make_async_remote_copy(
            src_ref=src, dst_ref=dst, send_sem=send.at[at], recv_sem=recv.at[at], device_id=to, device_id_type=MESH
        )

    barrier = pltpu.get_barrier_semaphore()
    everyone = [a_peer(r) for r in range(1, na)] + [group_peer(r) for r in range(1, group)] + [c_peer]
    for to in everyone:
        pl.semaphore_signal(barrier, inc=1, device_id=to, device_id_type=MESH)

    own_slot = kv.at[a, :, y, x]
    own = [
        pltpu.make_async_copy(src, dst, sem["own"].at[i])
        for i, (src, dst) in enumerate([
            (pos_ref, ids.at[0]), (doc_ref, ids.at[1]),
            (k_ref, kv.at[a, 0, y, x]), (v_ref, kv.at[a, 1, y, x]),
            (q_ref, raw.at[0, c]), (g_ref, raw.at[1, c]),
        ])
    ]
    for one in own:
        one.start()

    pl.semaphore_wait(barrier, len(everyone))

    def a_copy(step):
        return copy(own_slot, own_slot, "a", step, a_peer(step))

    def group_copies(step):
        block = kv.at[xor(a, step, a_bits), :, y, x]
        return [copy(block, block, "g", step * group + r, group_peer(r)) for r in range(1, group)]

    def send_all(copies):
        for one in copies:
            one.start()

    own[2].wait()
    own[3].wait()
    first = [a_copy(r) for r in range(1, na)]
    send_all(first)
    send_all(group_copies(0))

    share = [copy(q_ref, raw.at[0, c], "qg", 0, c_peer), copy(g_ref, raw.at[1, c], "qg", 1, c_peer)]
    for one in share:
        one.start()

    fields = docs + 1
    own[0].wait()
    own[1].wait()
    pos_own = ids[0]
    doc_own = ids[1]
    info[a, y, x, 0] = jnp.broadcast_to(pos_own[:, 0:1], (1, 128))
    for d in range(docs):
        tally = jnp.sum(jnp.where(doc_own == d, 1, 0), axis=1, keepdims=True)
        info[a, y, x, 1 + d] = jnp.broadcast_to(tally, (1, 128))
    info_slot = info.at[a, y, x]
    facts = [copy(info_slot, info_slot, "ginf", r, group_peer(r)) for r in range(1, group)]
    spare = 128 - 2 * rows
    pieces = [pos_own, doc_own] + ([jnp.zeros((1, spare), jnp.int32)] if spare else [])
    info_q = sem["info_q"]
    info_q[c] = jnp.concatenate(pieces, axis=1)
    id_share = copy(info_q.at[c], info_q.at[c], "idq", 0, c_peer)
    for one in facts + [id_share]:
        one.start()

    def relay(step):
        a_copy(step).wait_recv()
        send_all(group_copies(step))

    facts_a = [copy(info.at[a], info.at[a], "ainf", r, a_peer(r)) for r in range(1, na)]
    for one in facts:
        one.wait_recv()
    send_all(facts_a)
    for one in own[4:]:
        one.wait()
    for one in share + [id_share]:
        one.wait_recv()
    for k in range(CORES):
        for h in range(heads):
            at = k * lanes + h * rows
            qs[at : at + rows, :] = raw[0, k, :, h * 128 : (h + 1) * 128]
            gs[at : at + rows, :] = raw[1, k, :, h * 128 : (h + 1) * 128]
    for step in range(1, min(3, na)):
        relay(step)
    qt[...] = jnp.transpose(qs[...])
    gt[...] = jnp.transpose(gs[...])
    both = [info_q[k] for k in range(CORES)]
    pos_q = jnp.concatenate([one[:, :rows] for one in both for _ in range(heads)], axis=1)
    doc_q = jnp.concatenate([one[:, rows : 2 * rows] for one in both for _ in range(heads)], axis=1)
    wide = CORES * lanes
    stats[0] = jnp.full((1, wide), NEG_BIG, F32)
    stats[1] = jnp.zeros((1, wide), F32)
    stats[2] = jnp.zeros((1, wide), F32)
    dqt[...] = jnp.zeros(dqt.shape, F32)

    row_ids = lax.broadcasted_iota(jnp.int32, (rows, wide), 0)

    def widen(row):
        return jnp.concatenate([row] * (wide // 128), axis=1)

    def chunk_of(step, which):
        return kv[xor(a, step, a_bits), which].reshape(group * rows, 128)

    def look(step, carry):
        @pl.when((step >= 1) & (step + 2 < na))
        def _():
            relay(step + 2)

        @pl.when(step == 1)
        def _():
            for one in facts_a:
                one.wait_recv()

        for one in group_copies(step):
            one.wait_recv()

        scores = dot(chunk_of(step, 0), qt[...], 1, 0)
        dprobs = dot(chunk_of(step, 1), gt[...], 1, 0)
        old = stats[0]
        high = old
        at = xor(a, step, a_bits)
        for b in range(group):
            row = lambda f: widen(info[at, b // nx, b % nx, f])
            upper = pos_q - row(0)
            lower = jnp.zeros((1, wide), jnp.int32)
            for d in range(docs):
                lower = lower + jnp.where(doc_q > d, row(1 + d), 0)
            seen = (row_ids >= lower) & (row_ids <= upper)
            part = jnp.where(seen, scores[b * rows : (b + 1) * rows, :] * scale, NEG_BIG)
            sbuf[step, b * rows : (b + 1) * rows, :] = part
            high = jnp.maximum(high, jnp.max(part, axis=0, keepdims=True))
        dpbuf[step] = dprobs
        fade = jnp.exp2(old - high)
        weights = jnp.exp2(sbuf[step] - high)
        stats[0] = high
        stats[1] = stats[1] * fade + jnp.sum(weights, axis=0, keepdims=True)
        stats[2] = stats[2] * fade + jnp.sum(weights * dprobs, axis=0, keepdims=True)
        return carry

    lax.fori_loop(0, na, look, 0)

    stats_in = sem["stats_in"]
    swap = copy(stats, stats_in, "stat", 0, c_peer)
    swap.start()
    swap.wait_recv()
    high = jnp.maximum(stats[0], stats_in[0])
    here, there = jnp.exp2(stats[0] - high), jnp.exp2(stats_in[0] - high)
    denom = stats[1] * here + stats_in[1] * there
    log_total = high + jnp.log2(denom)
    row_dot = (stats[2] * here + stats_in[2] * there) / denom

    def sum_copies(step):
        found = []
        for r in range(1, group):
            yy, xx = group_place(r)
            at = step * group + r
            found.append(copy(g_out.at[step, :, yy, xx], g_in.at[at], "sum", at, group_peer(r)))
        return found

    def ra_copy(step):
        return copy(a_out.at[step], a_in.at[step], "ra", step, a_peer(step))

    def grads(step):
        probs = jnp.exp2(sbuf[step] - log_total)
        dscores = (probs * (dpbuf[step] - row_dot)).astype(BF16)
        dk = dot(dscores, qs[...], 1, 0) * inv_root
        dv = dot(probs.astype(BF16), gs[...], 1, 0)
        for which, one in enumerate((dk, dv)):
            one = one.reshape(SIDES, nx, rows, 128)
            g_out[step, which] = one.astype(BF16)
            acc[step, which] = one
        send_all(sum_copies(step))
        part = dot(chunk_of(step, 0), dscores, 0, 0)
        for k in range(CORES):
            dqt[k] += part[:, k * lanes : (k + 1) * lanes]

    def second(step):
        total = acc[step, :, y, x]
        for r, one in enumerate(sum_copies(step)):
            one.wait_recv()
            total = total + g_in[step * group + r + 1].astype(F32)
        a_own[step] = total

        @pl.when(step > 0)
        def _():
            a_out[step] = total.astype(BF16)
            ra_copy(step).start()

    def turn(i, carry):
        grads(na - 1 - i)

        @pl.when(i >= LAG)
        def _():
            second(na - 1 - i + LAG)

        return carry

    lax.fori_loop(0, na, turn, 0)
    dq_own = sem["dq_own"]
    swap_dq = copy(dqt.at[1 - c], dq_in, "dq", 0, c_peer)
    swap_dq.start()

    for step in range(min(LAG, na) - 1, 0, -1):
        second(step)
    swap_dq.wait_recv()
    dq = jnp.transpose(dqt[c] + dq_in[...]) * inv_root
    for h in range(heads):
        dq_own[:, h * 128 : (h + 1) * 128] = dq[h * rows : (h + 1) * rows, :]
    results = [
        pltpu.make_async_copy(src, dst, sem["out"].at[i])
        for i, (src, dst) in enumerate([(dq_own, dq_ref), (sem["dk_own"], dk_ref), (sem["dv_own"], dv_ref)])
    ]
    results[0].start()

    second(0)

    for one in first + share + [id_share] + facts + facts_a + [swap, swap_dq]:
        one.wait_send()

    def sent(step, carry):
        @pl.when(step > 0)
        def _():
            ra_copy(step).wait_send()

        for one in group_copies(step) + sum_copies(step):
            one.wait_send()
        return carry

    lax.fori_loop(0, na, sent, 0)

    def collect(step, carry):
        ra_copy(step).wait_recv()
        return carry + a_in[step].astype(F32)

    done = lax.fori_loop(1, na, collect, a_own[0])
    sem["dk_own"][...] = done[0]
    sem["dv_own"][...] = done[1]
    results[1].start()
    results[2].start()
    for one in results:
        one.wait()


def hand_over(*refs):
    count = (len(refs) - 1) // 2
    moves = [pltpu.make_async_copy(refs[i], refs[count + i], refs[-1].at[i]) for i in range(count)]
    for one in moves:
        one.start()
    for one in moves:
        one.wait()


def on_device(queries, key_vecs, value_vecs, out_grad, positions, documents):
    nx = lax.axis_size("head")
    na = lax.axis_size("ctx") // (CORES * SIDES)
    rows, width = queries.shape
    heads = width // 128
    seq = rows * nx * na * CORES * SIDES
    docs = max(2, seq // 1024)
    lanes, group = heads * rows, SIDES * nx
    chunk = group * rows
    wide = CORES * lanes
    dma = pltpu.SemaphoreType.DMA
    vmem = pltpu.VMEM
    copies = {
        "a": na, "g": na * group, "ginf": group, "ainf": na, "idq": 1, "qg": 2, "stat": 1,
        "sum": na * group, "ra": na, "dq": 1,
    }
    names, tail = [], []
    for name, count in copies.items():
        names += ["s_" + name, "r_" + name]
        tail += [dma((count,)), dma((count,))]
    names += ["own", "out", "info_q", "stats_in", "dq_own", "dk_own", "dv_own"]
    tail += [dma((6,)), dma((3,)), vmem((CORES, 1, 128), jnp.int32), vmem((3, 1, wide), F32)]
    tail += [vmem((rows, width), F32), vmem((rows, 128), F32), vmem((rows, 128), F32)]
    scratch = [
        vmem((2, CORES, rows, width), BF16),
        vmem((wide, 128), BF16),
        vmem((wide, 128), BF16),
        vmem((128, wide), BF16),
        vmem((128, wide), BF16),
        vmem((na, 2, SIDES, nx, rows, 128), BF16),
        vmem((na, SIDES, nx, docs + 1, 1, 128), jnp.int32),
        vmem((2, 1, rows), jnp.int32),
        vmem((na, chunk, wide), F32),
        vmem((na, chunk, wide), F32),
        vmem((3, 1, wide), F32),
        vmem((CORES, 128, lanes), F32),
        vmem((128, lanes), F32),
        vmem((na, 2, SIDES, nx, rows, 128), F32),
        vmem((na, 2, SIDES, nx, rows, 128), BF16),
        vmem((na * group, 2, rows, 128), BF16),
        vmem((na, 2, rows, 128), BF16),
        vmem((na, 2, rows, 128), BF16),
        vmem((na, 2, rows, 128), F32),
    ] + tail
    cfg = (nx, na, rows, heads, docs, names)
    far = pl.BlockSpec(memory_space=pltpu.HBM)
    pairs = lanes * seq
    shapes = (
        jax.ShapeDtypeStruct((rows, width), F32),
        jax.ShapeDtypeStruct((rows, 128), F32),
        jax.ShapeDtypeStruct((rows, 128), F32),
    )
    found = pl.pallas_call(
        functools.partial(kernel, cfg),
        out_shape=shapes,
        in_specs=[far] * 6,
        out_specs=(far, far, far),
        scratch_shapes=scratch,
        compiler_params=pltpu.CompilerParams(
            collective_id=0, has_side_effects=True, vmem_limit_bytes=64 * 1024 * 1024
        ),
        cost_estimate=pl.CostEstimate(
            flops=10 * pairs * 128, bytes_accessed=rows * width * 8, transcendentals=2 * pairs
        ),
    )(queries, key_vecs, value_vecs, out_grad, positions.reshape(1, rows), documents.reshape(1, rows))
    return pl.pallas_call(
        hand_over,
        out_shape=shapes,
        in_specs=[pl.BlockSpec(memory_space=pltpu.VMEM)] * 3,
        out_specs=(far, far, far),
        scratch_shapes=[dma((3,))],
        compiler_params=pltpu.CompilerParams(vmem_limit_bytes=64 * 1024 * 1024),
    )(*found)


def solution(mesh):
    tokens = P(("head", "ctx"), None)
    ids = P(("head", "ctx"))
    return jax.shard_map(
        on_device,
        mesh=mesh,
        in_specs=(tokens, tokens, tokens, tokens, ids, ids),
        out_specs=(tokens, tokens, tokens),
        check_vma=False,
    )
```

```python
import functools
import math

import jax
import jax.numpy as jnp
from jax import lax
from jax.experimental import pallas as pl
from jax.experimental.pallas import tpu as pltpu
from jax.sharding import PartitionSpec as P

MESH = pl.DeviceIdType.MESH
NEG_BIG = -1e30
CORES = 2
TILE = 256
LAG = 2
SIDES = 2
F32 = jnp.float32
BF16 = jnp.bfloat16


def dot(lhs, rhs, lhs_dim, rhs_dim):
    return lax.dot_general(
        lhs, rhs, (((lhs_dim,), (rhs_dim,)), ((), ())), preferred_element_type=F32
    )


def xor(left, right, bits):
    total = 0
    for b in range(bits):
        total = total + ((left // 2**b + right // 2**b) % 2) * 2**b
    return total


def kernel(
    cfg,
    q_ref, k_ref, v_ref, g_ref, pos_ref, doc_ref,
    dq_ref, dk_ref, dv_ref,
    raw, qs, gs, qt, gt, kv, info, ids, sbuf, dpbuf, stats, dqt, dq_in, acc, g_out, g_in, a_out, a_in, a_own,
    *sems,
):
    nx, na, rows, heads, docs, names = cfg
    sem = dict(zip(names, sems))
    lanes = heads * rows
    group = SIDES * nx
    x_bits, a_bits = (nx - 1).bit_length(), (na - 1).bit_length()
    inv_root = 1.0 / math.sqrt(128)
    scale = inv_root * math.log2(math.e)

    x = lax.axis_index("head")
    ctx = lax.axis_index("ctx")
    a, y, c = ctx // 4, (ctx // 2) % 2, ctx % 2

    def a_peer(r):
        return (x, xor(a, r, a_bits) * 4 + y * 2 + c)

    def group_place(r):
        return ((y + r // nx) % SIDES, xor(x, r % nx, x_bits))

    def group_peer(r):
        yy, xx = group_place(r)
        return (xx, a * 4 + yy * 2 + c)

    c_peer = (x, a * 4 + y * 2 + 1 - c)

    def copy(src, dst, name, at, to):
        send, recv = sem["s_" + name], sem["r_" + name]
        return pltpu.make_async_remote_copy(
            src_ref=src, dst_ref=dst, send_sem=send.at[at], recv_sem=recv.at[at], device_id=to, device_id_type=MESH
        )

    barrier = pltpu.get_barrier_semaphore()
    everyone = [a_peer(r) for r in range(1, na)] + [group_peer(r) for r in range(1, group)] + [c_peer]
    for to in everyone:
        pl.semaphore_signal(barrier, inc=1, device_id=to, device_id_type=MESH)

    own_slot = kv.at[a, :, y, x]
    own = [
        pltpu.make_async_copy(src, dst, sem["own"].at[i])
        for i, (src, dst) in enumerate([
            (pos_ref, ids.at[0]), (doc_ref, ids.at[1]),
            (k_ref, kv.at[a, 0, y, x]), (v_ref, kv.at[a, 1, y, x]),
            (q_ref, raw.at[0, c]), (g_ref, raw.at[1, c]),
        ])
    ]
    for one in own:
        one.start()

    pl.semaphore_wait(barrier, len(everyone))

    def a_copy(step):
        return copy(own_slot, own_slot, "a", step, a_peer(step))

    def group_copies(step):
        block = kv.at[xor(a, step, a_bits), :, y, x]
        return [copy(block, block, "g", step * group + r, group_peer(r)) for r in range(1, group)]

    def send_all(copies):
        for one in copies:
            one.start()

    own[2].wait()
    own[3].wait()
    first = [a_copy(r) for r in range(1, na)]
    send_all(first)
    send_all(group_copies(0))

    share = [copy(q_ref, raw.at[0, c], "qg", 0, c_peer), copy(g_ref, raw.at[1, c], "qg", 1, c_peer)]
    for one in share:
        one.start()

    fields = docs + 1
    own[0].wait()
    own[1].wait()
    pos_own = ids[0]
    doc_own = ids[1]
    info[a, y, x, 0] = jnp.broadcast_to(pos_own[:, 0:1], (1, 128))
    for d in range(docs):
        tally = jnp.sum(jnp.where(doc_own == d, 1, 0), axis=1, keepdims=True)
        info[a, y, x, 1 + d] = jnp.broadcast_to(tally, (1, 128))
    info_slot = info.at[a, y, x]
    facts = [copy(info_slot, info_slot, "ginf", r, group_peer(r)) for r in range(1, group)]
    spare = 128 - 2 * rows
    pieces = [pos_own, doc_own] + ([jnp.zeros((1, spare), jnp.int32)] if spare else [])
    info_q = sem["info_q"]
    info_q[c] = jnp.concatenate(pieces, axis=1)
    id_share = copy(info_q.at[c], info_q.at[c], "idq", 0, c_peer)
    for one in facts + [id_share]:
        one.start()

    def relay(step):
        a_copy(step).wait_recv()
        send_all(group_copies(step))

    facts_a = [copy(info.at[a], info.at[a], "ainf", r, a_peer(r)) for r in range(1, na)]
    for one in facts:
        one.wait_recv()
    send_all(facts_a)
    for one in own[4:]:
        one.wait()
    for one in share + [id_share]:
        one.wait_recv()
    for k in range(CORES):
        for h in range(heads):
            at = k * lanes + h * rows
            qs[at : at + rows, :] = raw[0, k, :, h * 128 : (h + 1) * 128]
            gs[at : at + rows, :] = raw[1, k, :, h * 128 : (h + 1) * 128]
    for step in range(1, min(3, na)):
        relay(step)
    qt[...] = jnp.transpose(qs[...])
    gt[...] = jnp.transpose(gs[...])
    both = [info_q[k] for k in range(CORES)]
    pos_q = jnp.concatenate([one[:, :rows] for one in both for _ in range(heads)], axis=1)
    doc_q = jnp.concatenate([one[:, rows : 2 * rows] for one in both for _ in range(heads)], axis=1)
    wide = CORES * lanes
    stats[0] = jnp.full((1, wide), NEG_BIG, F32)
    stats[1] = jnp.zeros((1, wide), F32)
    stats[2] = jnp.zeros((1, wide), F32)
    dqt[...] = jnp.zeros(dqt.shape, F32)

    tile = min(TILE, wide)
    tiles = [slice(t, t + tile) for t in range(0, wide, tile)]
    row_ids = lax.broadcasted_iota(jnp.int32, (rows, tile), 0)

    def widen(row):
        return jnp.concatenate([row] * (tile // 128), axis=1)

    def chunk_of(step, which):
        return kv[xor(a, step, a_bits), which].reshape(group * rows, 128)

    def look(step, carry):
        @pl.when((step >= 1) & (step + 2 < na))
        def _():
            relay(step + 2)

        @pl.when(step == 1)
        def _():
            for one in facts_a:
                one.wait_recv()

        for one in group_copies(step):
            one.wait_recv()

        keys, values = chunk_of(step, 0), chunk_of(step, 1)
        at = xor(a, step, a_bits)
        for cols in tiles:
            scores = dot(keys, qt[:, cols], 1, 0)
            old = stats[0, :, cols]
            high = old
            for b in range(group):
                row = lambda f: widen(info[at, b // nx, b % nx, f])
                upper = pos_q[:, cols] - row(0)
                lower = jnp.zeros((1, tile), jnp.int32)
                for d in range(docs):
                    lower = lower + jnp.where(doc_q[:, cols] > d, row(1 + d), 0)
                seen = (row_ids >= lower) & (row_ids <= upper)
                part = jnp.where(seen, scores[b * rows : (b + 1) * rows, :] * scale, NEG_BIG)
                sbuf[step, b * rows : (b + 1) * rows, cols] = part
                high = jnp.maximum(high, jnp.max(part, axis=0, keepdims=True))
            dprobs = dot(values, gt[:, cols], 1, 0)
            dpbuf[step, :, cols] = dprobs
            fade = jnp.exp2(old - high)
            weights = jnp.exp2(sbuf[step, :, cols] - high)
            stats[0, :, cols] = high
            stats[1, :, cols] = stats[1, :, cols] * fade + jnp.sum(weights, axis=0, keepdims=True)
            stats[2, :, cols] = stats[2, :, cols] * fade + jnp.sum(weights * dprobs, axis=0, keepdims=True)
        return carry

    lax.fori_loop(0, na, look, 0)

    stats_in = sem["stats_in"]
    swap = copy(stats, stats_in, "stat", 0, c_peer)
    swap.start()
    swap.wait_recv()
    high = jnp.maximum(stats[0], stats_in[0])
    here, there = jnp.exp2(stats[0] - high), jnp.exp2(stats_in[0] - high)
    denom = stats[1] * here + stats_in[1] * there
    log_total = high + jnp.log2(denom)
    row_dot = (stats[2] * here + stats_in[2] * there) / denom

    def sum_copies(step):
        found = []
        for r in range(1, group):
            yy, xx = group_place(r)
            at = step * group + r
            found.append(copy(g_out.at[step, :, yy, xx], g_in.at[at], "sum", at, group_peer(r)))
        return found

    def ra_copy(step):
        return copy(a_out.at[step], a_in.at[step], "ra", step, a_peer(step))

    def grads(step):
        keys = chunk_of(step, 0)
        for cols in tiles:
            probs = jnp.exp2(sbuf[step, :, cols] - log_total[:, cols])
            dscores = (probs * (dpbuf[step, :, cols] - row_dot[:, cols])).astype(BF16)
            sem["probs"][:, cols] = probs.astype(BF16)
            sem["dscores"][:, cols] = dscores
        dk = dot(sem["dscores"][...], qs[...], 1, 0) * inv_root
        dv = dot(sem["probs"][...], gs[...], 1, 0)
        for which, one in enumerate((dk, dv)):
            one = one.reshape(SIDES, nx, rows, 128)
            g_out[step, which] = one.astype(BF16)
            acc[step, which] = one
        send_all(sum_copies(step))
        for k in range(CORES):
            dqt[k] += dot(keys, sem["dscores"][:, k * lanes : (k + 1) * lanes], 0, 0)

    def second(step):
        total = acc[step, :, y, x]
        for r, one in enumerate(sum_copies(step)):
            one.wait_recv()
            total = total + g_in[step * group + r + 1].astype(F32)
        a_own[step] = total

        @pl.when(step > 0)
        def _():
            a_out[step] = total.astype(BF16)
            ra_copy(step).start()

    def turn(i, carry):
        grads(na - 1 - i)

        @pl.when(i >= LAG)
        def _():
            second(na - 1 - i + LAG)

        return carry

    lax.fori_loop(0, na, turn, 0)
    swap_dq = copy(dqt.at[1 - c], dq_in, "dq", 0, c_peer)
    swap_dq.start()

    for step in range(min(LAG, na) - 1, 0, -1):
        second(step)
    swap_dq.wait_recv()
    dq = jnp.transpose(dqt[c] + dq_in[...]) * inv_root
    for h in range(heads):
        dq_ref[:, h * 128 : (h + 1) * 128] = dq[h * rows : (h + 1) * rows, :]
    second(0)

    for one in first + share + [id_share] + facts + facts_a + [swap, swap_dq]:
        one.wait_send()

    def sent(step, carry):
        @pl.when(step > 0)
        def _():
            ra_copy(step).wait_send()

        for one in group_copies(step) + sum_copies(step):
            one.wait_send()
        return carry

    lax.fori_loop(0, na, sent, 0)

    def collect(step, carry):
        ra_copy(step).wait_recv()
        return carry + a_in[step].astype(F32)

    done = lax.fori_loop(1, na, collect, a_own[0])
    dk_ref[...] = done[0]
    dv_ref[...] = done[1]


def hand_over(*refs):
    count = (len(refs) - 1) // 2
    moves = [pltpu.make_async_copy(refs[i], refs[count + i], refs[-1].at[i]) for i in range(count)]
    for one in moves:
        one.start()
    for one in moves:
        one.wait()


def on_device(queries, key_vecs, value_vecs, out_grad, positions, documents):
    nx = lax.axis_size("head")
    na = lax.axis_size("ctx") // (CORES * SIDES)
    rows, width = queries.shape
    heads = width // 128
    seq = rows * nx * na * CORES * SIDES
    docs = max(2, seq // 1024)
    lanes, group = heads * rows, SIDES * nx
    chunk = group * rows
    wide = CORES * lanes
    dma = pltpu.SemaphoreType.DMA
    vmem = pltpu.VMEM
    copies = {
        "a": na, "g": na * group, "ginf": group, "ainf": na, "idq": 1, "qg": 2, "stat": 1,
        "sum": na * group, "ra": na, "dq": 1,
    }
    names, tail = [], []
    for name, count in copies.items():
        names += ["s_" + name, "r_" + name]
        tail += [dma((count,)), dma((count,))]
    names += ["own", "info_q", "stats_in", "probs", "dscores"]
    tail += [dma((6,)), vmem((CORES, 1, 128), jnp.int32), vmem((3, 1, wide), F32)]
    tail += [vmem((chunk, wide), BF16), vmem((chunk, wide), BF16)]
    scratch = [
        vmem((2, CORES, rows, width), BF16),
        vmem((wide, 128), BF16),
        vmem((wide, 128), BF16),
        vmem((128, wide), BF16),
        vmem((128, wide), BF16),
        vmem((na, 2, SIDES, nx, rows, 128), BF16),
        vmem((na, SIDES, nx, docs + 1, 1, 128), jnp.int32),
        vmem((2, 1, rows), jnp.int32),
        vmem((na, chunk, wide), F32),
        vmem((na, chunk, wide), F32),
        vmem((3, 1, wide), F32),
        vmem((CORES, 128, lanes), F32),
        vmem((128, lanes), F32),
        vmem((na, 2, SIDES, nx, rows, 128), F32),
        vmem((na, 2, SIDES, nx, rows, 128), BF16),
        vmem((na * group, 2, rows, 128), BF16),
        vmem((na, 2, rows, 128), BF16),
        vmem((na, 2, rows, 128), BF16),
        vmem((na, 2, rows, 128), F32),
    ] + tail
    cfg = (nx, na, rows, heads, docs, names)
    far = pl.BlockSpec(memory_space=pltpu.HBM)
    pairs = lanes * seq
    shapes = (
        jax.ShapeDtypeStruct((rows, width), F32),
        jax.ShapeDtypeStruct((rows, 128), F32),
        jax.ShapeDtypeStruct((rows, 128), F32),
    )
    near = pl.BlockSpec(memory_space=pltpu.VMEM)
    found = pl.pallas_call(
        functools.partial(kernel, cfg),
        out_shape=tuple(pltpu.VMEM(one.shape, one.dtype) for one in shapes),
        in_specs=[far] * 6,
        out_specs=(near, near, near),
        scratch_shapes=scratch,
        compiler_params=pltpu.CompilerParams(
            collective_id=0, has_side_effects=True, vmem_limit_bytes=63 * 1024 * 1024
        ),
        cost_estimate=pl.CostEstimate(
            flops=10 * pairs * 128, bytes_accessed=rows * width * 8, transcendentals=2 * pairs
        ),
    )(queries, key_vecs, value_vecs, out_grad, positions.reshape(1, rows), documents.reshape(1, rows))
    return pl.pallas_call(
        hand_over,
        out_shape=shapes,
        in_specs=[pl.BlockSpec(memory_space=pltpu.VMEM)] * 3,
        out_specs=(far, far, far),
        scratch_shapes=[dma((3,))],
        compiler_params=pltpu.CompilerParams(vmem_limit_bytes=1024 * 1024),
    )(*found)


def solution(mesh):
    tokens = P(("head", "ctx"), None)
    ids = P(("head", "ctx"))
    return jax.shard_map(
        on_device,
        mesh=mesh,
        in_specs=(tokens, tokens, tokens, tokens, ids, ids),
        out_specs=(tokens, tokens, tokens),
        check_vma=False,
    )
```

```python
import functools
import math

import jax
import jax.numpy as jnp
from jax import lax
from jax.experimental import pallas as pl
from jax.experimental.pallas import tpu as pltpu
from jax.sharding import PartitionSpec as P

MESH = pl.DeviceIdType.MESH
NEG_BIG = -1e30
CORES = 2
TILE = 256
FACTS = 16
LAG = 2
SIDES = 2
F32 = jnp.float32
BF16 = jnp.bfloat16


def dot(lhs, rhs, lhs_dim, rhs_dim):
    return lax.dot_general(
        lhs, rhs, (((lhs_dim,), (rhs_dim,)), ((), ())), preferred_element_type=F32
    )


def xor(left, right, bits):
    total = 0
    for b in range(bits):
        total = total + ((left // 2**b + right // 2**b) % 2) * 2**b
    return total


def kernel(
    cfg,
    q_ref, k_ref, v_ref, g_ref, pos_ref, doc_ref,
    dq_ref, dk_ref, dv_ref,
    raw, qs, gs, qt, gt, kv, ids, sbuf, dpbuf, stats, dqt, dq_in, acc, g_out, g_in, a_out, a_in, a_own,
    *sems,
):
    nx, na, rows, heads, docs, names = cfg
    sem = dict(zip(names, sems))
    lanes = heads * rows
    group = SIDES * nx
    x_bits, a_bits = (nx - 1).bit_length(), (na - 1).bit_length()
    inv_root = 1.0 / math.sqrt(128)
    scale = inv_root * math.log2(math.e)

    x = lax.axis_index("head")
    ctx = lax.axis_index("ctx")
    a, y, c = ctx // 4, (ctx // 2) % 2, ctx % 2

    def a_peer(r):
        return (x, xor(a, r, a_bits) * 4 + y * 2 + c)

    def group_place(r):
        return ((y + r // nx) % SIDES, xor(x, r % nx, x_bits))

    def group_peer(r):
        yy, xx = group_place(r)
        return (xx, a * 4 + yy * 2 + c)

    c_peer = (x, a * 4 + y * 2 + 1 - c)

    def copy(src, dst, name, at, to):
        send, recv = sem["s_" + name], sem["r_" + name]
        return pltpu.make_async_remote_copy(
            src_ref=src, dst_ref=dst, send_sem=send.at[at], recv_sem=recv.at[at], device_id=to, device_id_type=MESH
        )

    barrier = pltpu.get_barrier_semaphore()
    everyone = [a_peer(r) for r in range(1, na)] + [group_peer(r) for r in range(1, group)] + [c_peer]
    for to in everyone:
        pl.semaphore_signal(barrier, inc=1, device_id=to, device_id_type=MESH)

    own_slot = kv.at[a, y, x]
    own = [
        pltpu.make_async_copy(src, dst, sem["own"].at[i])
        for i, (src, dst) in enumerate([
            (pos_ref, ids.at[0]), (doc_ref, ids.at[1]),
            (k_ref, kv.at[a, y, x, pl.ds(0, rows)]), (v_ref, kv.at[a, y, x, pl.ds(rows, rows)]),
            (q_ref, raw.at[0, c]), (g_ref, raw.at[1, c]),
        ])
    ]
    for one in own:
        one.start()

    own[0].wait()
    own[1].wait()
    pos_own = ids[0].astype(F32)
    doc_own = ids[1].astype(F32)
    coarse = jnp.floor(pos_own[:, 0:1] * (1.0 / 128.0))
    fields = [coarse, pos_own[:, 0:1] - coarse * 128.0]
    for d in range(docs):
        fields.append(jnp.sum(jnp.where(doc_own == d, 1.0, 0.0), axis=1, keepdims=True))
    field_ids = lax.broadcasted_iota(jnp.int32, (FACTS, 128), 0)
    table = jnp.zeros((FACTS, 128), F32)
    for f, one in enumerate(fields):
        table = jnp.where(field_ids == f, one, table)
    kv[a, y, x, 2 * rows :, :] = table.astype(BF16)

    pl.semaphore_wait(barrier, len(everyone))

    def a_copy(step):
        return copy(own_slot, own_slot, "a", step, a_peer(step))

    def group_copies(step):
        block = kv.at[xor(a, step, a_bits), y, x]
        return [copy(block, block, "g", step * group + r, group_peer(r)) for r in range(1, group)]

    def send_all(copies):
        for one in copies:
            one.start()

    own[2].wait()
    own[3].wait()
    first = [a_copy(r) for r in range(1, na)]
    send_all(first)
    send_all(group_copies(0))

    share = [copy(q_ref, raw.at[0, c], "qg", 0, c_peer), copy(g_ref, raw.at[1, c], "qg", 1, c_peer)]
    for one in share:
        one.start()

    spare = 128 - 2 * rows
    pieces = [pos_own, doc_own] + ([jnp.zeros((1, spare), F32)] if spare else [])
    info_q = sem["info_q"]
    info_q[c] = jnp.concatenate(pieces, axis=1)
    id_share = copy(info_q.at[c], info_q.at[c], "idq", 0, c_peer)
    id_share.start()

    def relay(step):
        a_copy(step).wait_recv()
        send_all(group_copies(step))

    for one in own[4:]:
        one.wait()
    for one in share + [id_share]:
        one.wait_recv()
    for k in range(CORES):
        for h in range(heads):
            at = k * lanes + h * rows
            qs[at : at + rows, :] = raw[0, k, :, h * 128 : (h + 1) * 128]
            gs[at : at + rows, :] = raw[1, k, :, h * 128 : (h + 1) * 128]
    for step in range(1, min(3, na)):
        relay(step)
    qt[...] = jnp.transpose(qs[...])
    gt[...] = jnp.transpose(gs[...])
    both = [info_q[k] for k in range(CORES)]
    pos_q = jnp.concatenate([one[:, :rows] for one in both for _ in range(heads)], axis=1)
    doc_q = jnp.concatenate([one[:, rows : 2 * rows] for one in both for _ in range(heads)], axis=1)
    wide = CORES * lanes
    stats[0] = jnp.full((1, wide), NEG_BIG, F32)
    stats[1] = jnp.zeros((1, wide), F32)
    stats[2] = jnp.zeros((1, wide), F32)
    dqt[...] = jnp.zeros(dqt.shape, F32)

    tile = min(TILE, wide)
    tiles = [slice(t, t + tile) for t in range(0, wide, tile)]
    row_ids = lax.broadcasted_iota(jnp.int32, (rows, tile), 0).astype(F32)

    def widen(row):
        return jnp.concatenate([row] * (tile // 128), axis=1)

    def chunk_of(step, which):
        part = slice(which * rows, (which + 1) * rows)
        return kv[xor(a, step, a_bits), :, :, part, :].reshape(group * rows, 128)

    def look(step, carry):
        @pl.when((step >= 1) & (step + 2 < na))
        def _():
            relay(step + 2)

        for one in group_copies(step):
            one.wait_recv()

        keys, values = chunk_of(step, 0), chunk_of(step, 1)
        at = xor(a, step, a_bits)
        tables = [kv[at, b // nx, b % nx, 2 * rows :, :].astype(F32) for b in range(group)]
        for cols in tiles:
            scores = dot(keys, qt[:, cols], 1, 0)
            old = stats[0, :, cols]
            high = old
            for b in range(group):
                row = lambda f: widen(tables[b][f : f + 1, :])
                upper = pos_q[:, cols] - row(0) * 128.0 - row(1)
                lower = jnp.zeros((1, tile), F32)
                for d in range(docs):
                    lower = lower + jnp.where(doc_q[:, cols] > d, row(2 + d), 0.0)
                seen = (row_ids >= lower) & (row_ids <= upper)
                part = jnp.where(seen, scores[b * rows : (b + 1) * rows, :] * scale, NEG_BIG)
                sbuf[step, b * rows : (b + 1) * rows, cols] = part
                high = jnp.maximum(high, jnp.max(part, axis=0, keepdims=True))
            dprobs = dot(values, gt[:, cols], 1, 0)
            dpbuf[step, :, cols] = dprobs
            fade = jnp.exp2(old - high)
            weights = jnp.exp2(sbuf[step, :, cols] - high)
            stats[0, :, cols] = high
            stats[1, :, cols] = stats[1, :, cols] * fade + jnp.sum(weights, axis=0, keepdims=True)
            stats[2, :, cols] = stats[2, :, cols] * fade + jnp.sum(weights * dprobs, axis=0, keepdims=True)
        return carry

    lax.fori_loop(0, na, look, 0)

    stats_in = sem["stats_in"]
    swap = copy(stats, stats_in, "stat", 0, c_peer)
    swap.start()
    swap.wait_recv()
    high = jnp.maximum(stats[0], stats_in[0])
    here, there = jnp.exp2(stats[0] - high), jnp.exp2(stats_in[0] - high)
    denom = stats[1] * here + stats_in[1] * there
    log_total = high + jnp.log2(denom)
    row_dot = (stats[2] * here + stats_in[2] * there) / denom

    def sum_copies(step):
        found = []
        for r in range(1, group):
            yy, xx = group_place(r)
            at = step * group + r
            found.append(copy(g_out.at[step, :, yy, xx], g_in.at[at], "sum", at, group_peer(r)))
        return found

    def ra_copy(step):
        return copy(a_out.at[step], a_in.at[step], "ra", step, a_peer(step))

    def grads(step):
        keys_t = jnp.transpose(chunk_of(step, 0))
        for cols in tiles:
            probs = jnp.exp2(sbuf[step, :, cols] - log_total[:, cols])
            dscores = (probs * (dpbuf[step, :, cols] - row_dot[:, cols])).astype(BF16)
            sem["probs"][:, cols] = probs.astype(BF16)
            sem["dscores"][:, cols] = dscores
        dk = dot(sem["dscores"][...], qs[...], 1, 0) * inv_root
        dv = dot(sem["probs"][...], gs[...], 1, 0)
        for which, one in enumerate((dk, dv)):
            one = one.reshape(SIDES, nx, rows, 128)
            g_out[step, which] = one.astype(BF16)
            acc[step, which] = one
        send_all(sum_copies(step))
        for k in range(CORES):
            dqt[k] += dot(keys_t, sem["dscores"][:, k * lanes : (k + 1) * lanes], 1, 0)

    def second(step):
        total = acc[step, :, y, x]
        for r, one in enumerate(sum_copies(step)):
            one.wait_recv()
            total = total + g_in[step * group + r + 1].astype(F32)
        a_own[step] = total

        @pl.when(step > 0)
        def _():
            a_out[step] = total.astype(BF16)
            ra_copy(step).start()

    def turn(i, carry):
        grads(na - 1 - i)

        @pl.when(i >= LAG)
        def _():
            second(na - 1 - i + LAG)

        return carry

    lax.fori_loop(0, na, turn, 0)
    swap_dq = copy(dqt.at[1 - c], dq_in, "dq", 0, c_peer)
    swap_dq.start()

    for step in range(min(LAG, na) - 1, 0, -1):
        second(step)
    swap_dq.wait_recv()
    dq = jnp.transpose(dqt[c] + dq_in[...]) * inv_root
    for h in range(heads):
        dq_ref[:, h * 128 : (h + 1) * 128] = dq[h * rows : (h + 1) * rows, :]
    second(0)

    for one in first + share + [id_share] + [swap, swap_dq]:
        one.wait_send()

    def sent(step, carry):
        @pl.when(step > 0)
        def _():
            ra_copy(step).wait_send()

        for one in group_copies(step) + sum_copies(step):
            one.wait_send()
        return carry

    lax.fori_loop(0, na, sent, 0)

    def collect(step, carry):
        ra_copy(step).wait_recv()
        return carry + a_in[step].astype(F32)

    done = lax.fori_loop(1, na, collect, a_own[0])
    dk_ref[...] = done[0]
    dv_ref[...] = done[1]


def hand_over(*refs):
    count = (len(refs) - 1) // 2
    moves = [pltpu.make_async_copy(refs[i], refs[count + i], refs[-1].at[i]) for i in range(count)]
    for one in moves:
        one.start()
    for one in moves:
        one.wait()


def on_device(queries, key_vecs, value_vecs, out_grad, positions, documents):
    nx = lax.axis_size("head")
    na = lax.axis_size("ctx") // (CORES * SIDES)
    rows, width = queries.shape
    heads = width // 128
    seq = rows * nx * na * CORES * SIDES
    docs = max(2, seq // 1024)
    lanes, group = heads * rows, SIDES * nx
    chunk = group * rows
    wide = CORES * lanes
    dma = pltpu.SemaphoreType.DMA
    vmem = pltpu.VMEM
    copies = {
        "a": na, "g": na * group, "idq": 1, "qg": 2, "stat": 1,
        "sum": na * group, "ra": na, "dq": 1,
    }
    names, tail = [], []
    for name, count in copies.items():
        names += ["s_" + name, "r_" + name]
        tail += [dma((count,)), dma((count,))]
    names += ["own", "info_q", "stats_in", "probs", "dscores"]
    tail += [dma((6,)), vmem((CORES, 1, 128), F32), vmem((3, 1, wide), F32)]
    tail += [vmem((chunk, wide), BF16), vmem((chunk, wide), BF16)]
    scratch = [
        vmem((2, CORES, rows, width), BF16),
        vmem((wide, 128), BF16),
        vmem((wide, 128), BF16),
        vmem((128, wide), BF16),
        vmem((128, wide), BF16),
        vmem((na, SIDES, nx, 2 * rows + FACTS, 128), BF16),
        vmem((2, 1, rows), jnp.int32),
        vmem((na, chunk, wide), F32),
        vmem((na, chunk, wide), F32),
        vmem((3, 1, wide), F32),
        vmem((CORES, 128, lanes), F32),
        vmem((128, lanes), F32),
        vmem((na, 2, SIDES, nx, rows, 128), F32),
        vmem((na, 2, SIDES, nx, rows, 128), BF16),
        vmem((na * group, 2, rows, 128), BF16),
        vmem((na, 2, rows, 128), BF16),
        vmem((na, 2, rows, 128), BF16),
        vmem((na, 2, rows, 128), F32),
    ] + tail
    cfg = (nx, na, rows, heads, docs, names)
    far = pl.BlockSpec(memory_space=pltpu.HBM)
    pairs = lanes * seq
    shapes = (
        jax.ShapeDtypeStruct((rows, width), F32),
        jax.ShapeDtypeStruct((rows, 128), F32),
        jax.ShapeDtypeStruct((rows, 128), F32),
    )
    near = pl.BlockSpec(memory_space=pltpu.VMEM)
    found = pl.pallas_call(
        functools.partial(kernel, cfg),
        out_shape=tuple(pltpu.VMEM(one.shape, one.dtype) for one in shapes),
        in_specs=[far] * 6,
        out_specs=(near, near, near),
        scratch_shapes=scratch,
        compiler_params=pltpu.CompilerParams(
            collective_id=0, has_side_effects=True, vmem_limit_bytes=63 * 1024 * 1024
        ),
        cost_estimate=pl.CostEstimate(
            flops=10 * pairs * 128, bytes_accessed=rows * width * 8, transcendentals=2 * pairs
        ),
    )(queries, key_vecs, value_vecs, out_grad, positions.reshape(1, rows), documents.reshape(1, rows))
    return pl.pallas_call(
        hand_over,
        out_shape=shapes,
        in_specs=[pl.BlockSpec(memory_space=pltpu.VMEM)] * 3,
        out_specs=(far, far, far),
        scratch_shapes=[dma((3,))],
        compiler_params=pltpu.CompilerParams(vmem_limit_bytes=1024 * 1024),
    )(*found)


def solution(mesh):
    tokens = P(("head", "ctx"), None)
    ids = P(("head", "ctx"))
    return jax.shard_map(
        on_device,
        mesh=mesh,
        in_specs=(tokens, tokens, tokens, tokens, ids, ids),
        out_specs=(tokens, tokens, tokens),
        check_vma=False,
    )
```

```python
import functools
import math

import jax
import jax.numpy as jnp
from jax import lax
from jax.experimental import pallas as pl
from jax.experimental.pallas import tpu as pltpu
from jax.sharding import PartitionSpec as P

MESH = pl.DeviceIdType.MESH
NEG_BIG = -1e30
CORES = 2
TILE = 256
FACTS = 16
LAG = 2
SIDES = 2
F32 = jnp.float32
BF16 = jnp.bfloat16


def dot(lhs, rhs, lhs_dim, rhs_dim):
    return lax.dot_general(
        lhs, rhs, (((lhs_dim,), (rhs_dim,)), ((), ())), preferred_element_type=F32
    )


def xor(left, right, bits):
    total = 0
    for b in range(bits):
        total = total + ((left // 2**b + right // 2**b) % 2) * 2**b
    return total


def kernel(
    cfg,
    q_ref, k_ref, v_ref, g_ref, pos_ref, doc_ref,
    dq_ref, dk_ref, dv_ref,
    raw, qs, gs, qt, gt, kv, ids, sbuf, dpbuf, stats, dqt, dq_in, acc, g_out, g_in, a_out, a_in, a_own,
    *sems,
):
    nx, na, rows, heads, docs, names = cfg
    sem = dict(zip(names, sems))
    lanes = heads * rows
    group = SIDES * nx
    x_bits, a_bits = (nx - 1).bit_length(), (na - 1).bit_length()
    inv_root = 1.0 / math.sqrt(128)
    scale = inv_root * math.log2(math.e)

    x = lax.axis_index("head")
    ctx = lax.axis_index("ctx")
    a, y, c = ctx // 4, (ctx // 2) % 2, ctx % 2

    def a_peer(r):
        return (x, xor(a, r, a_bits) * 4 + y * 2 + c)

    def group_place(r):
        return ((y + r // nx) % SIDES, xor(x, r % nx, x_bits))

    def group_peer(r):
        yy, xx = group_place(r)
        return (xx, a * 4 + yy * 2 + c)

    c_peer = (x, a * 4 + y * 2 + 1 - c)

    def copy(src, dst, name, at, to):
        send, recv = sem["s_" + name], sem["r_" + name]
        return pltpu.make_async_remote_copy(
            src_ref=src, dst_ref=dst, send_sem=send.at[at], recv_sem=recv.at[at], device_id=to, device_id_type=MESH
        )

    barrier = pltpu.get_barrier_semaphore()
    everyone = [a_peer(r) for r in range(1, na)] + [group_peer(r) for r in range(1, group)] + [c_peer]
    for to in everyone:
        pl.semaphore_signal(barrier, inc=1, device_id=to, device_id_type=MESH)

    own_slot = kv.at[a, y, x]
    own = [
        pltpu.make_async_copy(src, dst, sem["own"].at[i])
        for i, (src, dst) in enumerate([
            (pos_ref, ids.at[0]), (doc_ref, ids.at[1]),
            (k_ref, kv.at[a, y, x, pl.ds(0, rows)]), (v_ref, kv.at[a, y, x, pl.ds(rows, rows)]),
            (q_ref, raw.at[0, c]), (g_ref, raw.at[1, c]),
        ])
    ]
    for one in own:
        one.start()

    own[0].wait()
    own[1].wait()
    pos_own = ids[0].astype(F32)
    doc_own = ids[1].astype(F32)
    coarse = jnp.floor(pos_own[:, 0:1] * (1.0 / 128.0))
    fields = [coarse, pos_own[:, 0:1] - coarse * 128.0]
    for d in range(docs):
        fields.append(jnp.sum(jnp.where(doc_own == d, 1.0, 0.0), axis=1, keepdims=True))
    field_ids = lax.broadcasted_iota(jnp.int32, (FACTS, 128), 0)
    table = jnp.zeros((FACTS, 128), F32)
    for f, one in enumerate(fields):
        table = jnp.where(field_ids == f, one, table)
    kv[a, y, x, 2 * rows :, :] = table.astype(BF16)

    pl.semaphore_wait(barrier, len(everyone))

    def a_copy(step):
        return copy(own_slot, own_slot, "a", step, a_peer(step))

    def group_copies(step):
        block = kv.at[xor(a, step, a_bits), y, x]
        return [copy(block, block, "g", step * group + r, group_peer(r)) for r in range(1, group)]

    def send_all(copies):
        for one in copies:
            one.start()

    own[2].wait()
    own[3].wait()
    first = [a_copy(r) for r in range(1, na)]
    send_all(first)
    send_all(group_copies(0))

    share = [copy(q_ref, raw.at[0, c], "qg", 0, c_peer), copy(g_ref, raw.at[1, c], "qg", 1, c_peer)]
    for one in share:
        one.start()

    spare = 128 - 2 * rows
    pieces = [pos_own, doc_own] + ([jnp.zeros((1, spare), F32)] if spare else [])
    info_q = sem["info_q"]
    info_q[c] = jnp.concatenate(pieces, axis=1)
    id_share = copy(info_q.at[c], info_q.at[c], "idq", 0, c_peer)
    id_share.start()

    def relay(step):
        a_copy(step).wait_recv()
        send_all(group_copies(step))

    def lay_out(core):
        base = core * lanes
        for h in range(heads):
            at = pl.ds(pl.multiple_of(base + h * rows, rows), rows)
            qs[at, :] = raw[0, core, :, h * 128 : (h + 1) * 128]
            gs[at, :] = raw[1, core, :, h * 128 : (h + 1) * 128]
        span = pl.ds(pl.multiple_of(base, lanes), lanes)
        qt[:, span] = jnp.transpose(qs[span, :])
        gt[:, span] = jnp.transpose(gs[span, :])

    for one in own[4:]:
        one.wait()
    lay_out(c)
    if na > 1:
        relay(1)
    for one in share + [id_share]:
        one.wait_recv()
    lay_out(1 - c)
    if na > 2:
        relay(2)
    both = [info_q[k] for k in range(CORES)]
    pos_q = jnp.concatenate([one[:, :rows] for one in both for _ in range(heads)], axis=1)
    doc_q = jnp.concatenate([one[:, rows : 2 * rows] for one in both for _ in range(heads)], axis=1)
    wide = CORES * lanes
    stats[0] = jnp.full((1, wide), NEG_BIG, F32)
    stats[1] = jnp.zeros((1, wide), F32)
    stats[2] = jnp.zeros((1, wide), F32)
    dqt[...] = jnp.zeros(dqt.shape, F32)

    tile = min(TILE, wide)
    tiles = [slice(t, t + tile) for t in range(0, wide, tile)]
    row_ids = lax.broadcasted_iota(jnp.int32, (rows, tile), 0).astype(F32)

    def widen(row):
        return jnp.concatenate([row] * (tile // 128), axis=1)

    def chunk_of(step, which):
        part = slice(which * rows, (which + 1) * rows)
        return kv[xor(a, step, a_bits), :, :, part, :].reshape(group * rows, 128)

    def look(step, carry):
        @pl.when((step >= 1) & (step + 2 < na))
        def _():
            relay(step + 2)

        for one in group_copies(step):
            one.wait_recv()

        keys, values = chunk_of(step, 0), chunk_of(step, 1)
        at = xor(a, step, a_bits)
        tables = [kv[at, b // nx, b % nx, 2 * rows :, :].astype(F32) for b in range(group)]
        for cols in tiles:
            scores = dot(keys, qt[:, cols], 1, 0)
            old = stats[0, :, cols]
            high = old
            for b in range(group):
                row = lambda f: widen(tables[b][f : f + 1, :])
                upper = pos_q[:, cols] - row(0) * 128.0 - row(1)
                lower = jnp.zeros((1, tile), F32)
                for d in range(docs):
                    lower = lower + jnp.where(doc_q[:, cols] > d, row(2 + d), 0.0)
                seen = (row_ids >= lower) & (row_ids <= upper)
                part = jnp.where(seen, scores[b * rows : (b + 1) * rows, :] * scale, NEG_BIG)
                sbuf[step, b * rows : (b + 1) * rows, cols] = part
                high = jnp.maximum(high, jnp.max(part, axis=0, keepdims=True))
            dprobs = dot(values, gt[:, cols], 1, 0)
            dpbuf[step, :, cols] = dprobs
            fade = jnp.exp2(old - high)
            weights = jnp.exp2(sbuf[step, :, cols] - high)
            stats[0, :, cols] = high
            stats[1, :, cols] = stats[1, :, cols] * fade + jnp.sum(weights, axis=0, keepdims=True)
            stats[2, :, cols] = stats[2, :, cols] * fade + jnp.sum(weights * dprobs, axis=0, keepdims=True)
        return carry

    lax.fori_loop(0, na, look, 0)

    stats_in = sem["stats_in"]
    swap = copy(stats, stats_in, "stat", 0, c_peer)
    swap.start()
    swap.wait_recv()
    high = jnp.maximum(stats[0], stats_in[0])
    here, there = jnp.exp2(stats[0] - high), jnp.exp2(stats_in[0] - high)
    denom = stats[1] * here + stats_in[1] * there
    log_total = high + jnp.log2(denom)
    row_dot = (stats[2] * here + stats_in[2] * there) / denom

    def sum_copies(step):
        found = []
        for r in range(1, group):
            yy, xx = group_place(r)
            at = step * group + r
            found.append(copy(g_out.at[step, :, yy, xx], g_in.at[at], "sum", at, group_peer(r)))
        return found

    def ra_copy(step):
        return copy(a_out.at[step], a_in.at[step], "ra", step, a_peer(step))

    def grads(step):
        keys_t = jnp.transpose(chunk_of(step, 0))
        for cols in tiles:
            probs = jnp.exp2(sbuf[step, :, cols] - log_total[:, cols])
            dscores = (probs * (dpbuf[step, :, cols] - row_dot[:, cols])).astype(BF16)
            sem["probs"][:, cols] = probs.astype(BF16)
            sem["dscores"][:, cols] = dscores
        dk = dot(sem["dscores"][...], qs[...], 1, 0)
        dv = dot(sem["probs"][...], gs[...], 1, 0)
        for which, one in enumerate((dk, dv)):
            one = one.reshape(SIDES, nx, rows, 128)
            g_out[step, which] = one.astype(BF16)
            acc[step, which] = one
        send_all(sum_copies(step))
        for k in range(CORES):
            dqt[k] += dot(keys_t, sem["dscores"][:, k * lanes : (k + 1) * lanes], 1, 0)

    def second(step):
        total = acc[step, :, y, x]
        for r, one in enumerate(sum_copies(step)):
            one.wait_recv()
            total = total + g_in[step * group + r + 1].astype(F32)
        a_own[step] = total

        @pl.when(step > 0)
        def _():
            a_out[step] = total.astype(BF16)
            ra_copy(step).start()

    def turn(i, carry):
        grads(na - 1 - i)

        @pl.when(i >= LAG)
        def _():
            second(na - 1 - i + LAG)

        return carry

    lax.fori_loop(0, na, turn, 0)
    swap_dq = copy(dqt.at[1 - c], dq_in, "dq", 0, c_peer)
    swap_dq.start()

    for step in range(min(LAG, na) - 1, 0, -1):
        second(step)
    swap_dq.wait_recv()
    dq = jnp.transpose(dqt[c] + dq_in[...]) * inv_root
    for h in range(heads):
        dq_ref[:, h * 128 : (h + 1) * 128] = dq[h * rows : (h + 1) * rows, :]
    second(0)

    for one in first + share + [id_share] + [swap, swap_dq]:
        one.wait_send()

    def sent(step, carry):
        @pl.when(step > 0)
        def _():
            ra_copy(step).wait_send()

        for one in group_copies(step) + sum_copies(step):
            one.wait_send()
        return carry

    lax.fori_loop(0, na, sent, 0)

    def collect(step, carry):
        ra_copy(step).wait_recv()
        return carry + a_in[step].astype(F32)

    done = lax.fori_loop(1, na, collect, a_own[0])
    dk_ref[...] = done[0] * inv_root
    dv_ref[...] = done[1]


def hand_over(*refs):
    count = (len(refs) - 1) // 2
    moves = [pltpu.make_async_copy(refs[i], refs[count + i], refs[-1].at[i]) for i in range(count)]
    for one in moves:
        one.start()
    for one in moves:
        one.wait()


def on_device(queries, key_vecs, value_vecs, out_grad, positions, documents):
    nx = lax.axis_size("head")
    na = lax.axis_size("ctx") // (CORES * SIDES)
    rows, width = queries.shape
    heads = width // 128
    seq = rows * nx * na * CORES * SIDES
    docs = max(2, seq // 1024)
    lanes, group = heads * rows, SIDES * nx
    chunk = group * rows
    wide = CORES * lanes
    dma = pltpu.SemaphoreType.DMA
    vmem = pltpu.VMEM
    copies = {
        "a": na, "g": na * group, "idq": 1, "qg": 2, "stat": 1,
        "sum": na * group, "ra": na, "dq": 1,
    }
    names, tail = [], []
    for name, count in copies.items():
        names += ["s_" + name, "r_" + name]
        tail += [dma((count,)), dma((count,))]
    names += ["own", "info_q", "stats_in", "probs", "dscores"]
    tail += [dma((6,)), vmem((CORES, 1, 128), F32), vmem((3, 1, wide), F32)]
    tail += [vmem((chunk, wide), BF16), vmem((chunk, wide), BF16)]
    scratch = [
        vmem((2, CORES, rows, width), BF16),
        vmem((wide, 128), BF16),
        vmem((wide, 128), BF16),
        vmem((128, wide), BF16),
        vmem((128, wide), BF16),
        vmem((na, SIDES, nx, 2 * rows + FACTS, 128), BF16),
        vmem((2, 1, rows), jnp.int32),
        vmem((na, chunk, wide), F32),
        vmem((na, chunk, wide), F32),
        vmem((3, 1, wide), F32),
        vmem((CORES, 128, lanes), F32),
        vmem((128, lanes), F32),
        vmem((na, 2, SIDES, nx, rows, 128), F32),
        vmem((na, 2, SIDES, nx, rows, 128), BF16),
        vmem((na * group, 2, rows, 128), BF16),
        vmem((na, 2, rows, 128), BF16),
        vmem((na, 2, rows, 128), BF16),
        vmem((na, 2, rows, 128), F32),
    ] + tail
    cfg = (nx, na, rows, heads, docs, names)
    far = pl.BlockSpec(memory_space=pltpu.HBM)
    pairs = lanes * seq
    shapes = (
        jax.ShapeDtypeStruct((rows, width), F32),
        jax.ShapeDtypeStruct((rows, 128), F32),
        jax.ShapeDtypeStruct((rows, 128), F32),
    )
    near = pl.BlockSpec(memory_space=pltpu.VMEM)
    found = pl.pallas_call(
        functools.partial(kernel, cfg),
        out_shape=tuple(pltpu.VMEM(one.shape, one.dtype) for one in shapes),
        in_specs=[far] * 6,
        out_specs=(near, near, near),
        scratch_shapes=scratch,
        compiler_params=pltpu.CompilerParams(
            collective_id=0, has_side_effects=True, vmem_limit_bytes=63 * 1024 * 1024
        ),
        cost_estimate=pl.CostEstimate(
            flops=10 * pairs * 128, bytes_accessed=rows * width * 8, transcendentals=2 * pairs
        ),
    )(queries, key_vecs, value_vecs, out_grad, positions.reshape(1, rows), documents.reshape(1, rows))
    return pl.pallas_call(
        hand_over,
        out_shape=shapes,
        in_specs=[pl.BlockSpec(memory_space=pltpu.VMEM)] * 3,
        out_specs=(far, far, far),
        scratch_shapes=[dma((3,))],
        compiler_params=pltpu.CompilerParams(vmem_limit_bytes=1024 * 1024),
    )(*found)


def solution(mesh):
    tokens = P(("head", "ctx"), None)
    ids = P(("head", "ctx"))
    return jax.shard_map(
        on_device,
        mesh=mesh,
        in_specs=(tokens, tokens, tokens, tokens, ids, ids),
        out_specs=(tokens, tokens, tokens),
        check_vma=False,
    )
```

```python
import functools
import math

import jax
import jax.numpy as jnp
from jax import lax
from jax.experimental import pallas as pl
from jax.experimental.pallas import tpu as pltpu
from jax.sharding import PartitionSpec as P

MESH = pl.DeviceIdType.MESH
NEG_BIG = -1e30
CORES = 2
TILE = 256
FACTS = 16
LAG = 2
SIDES = 2
F32 = jnp.float32
BF16 = jnp.bfloat16


def dot(lhs, rhs, lhs_dim, rhs_dim):
    return lax.dot_general(
        lhs, rhs, (((lhs_dim,), (rhs_dim,)), ((), ())), preferred_element_type=F32
    )


def xor(left, right, bits):
    total = 0
    for b in range(bits):
        total = total + ((left // 2**b + right // 2**b) % 2) * 2**b
    return total


def kernel(
    cfg,
    q_ref, k_ref, v_ref, g_ref, pos_ref, doc_ref,
    dq_ref, dk_ref, dv_ref,
    raw, qs, gs, qt, gt, kv, ids, sbuf, dpbuf, stats, dqt, dq_in, acc, g_out, g_in, a_out, a_in, a_own,
    *sems,
):
    nx, na, rows, heads, docs, names = cfg
    sem = dict(zip(names, sems))
    lanes = heads * rows
    group = SIDES * nx
    x_bits, a_bits = (nx - 1).bit_length(), (na - 1).bit_length()
    inv_root = 1.0 / math.sqrt(128)
    scale = inv_root * math.log2(math.e)

    x = lax.axis_index("head")
    ctx = lax.axis_index("ctx")
    a, y, c = ctx // 4, (ctx // 2) % 2, ctx % 2

    def a_peer(r):
        return (x, xor(a, r, a_bits) * 4 + y * 2 + c)

    def group_place(r):
        return ((y + r // nx) % SIDES, xor(x, r % nx, x_bits))

    def group_peer(r):
        yy, xx = group_place(r)
        return (xx, a * 4 + yy * 2 + c)

    c_peer = (x, a * 4 + y * 2 + 1 - c)

    def copy(src, dst, name, at, to):
        send, recv = sem["s_" + name], sem["r_" + name]
        return pltpu.make_async_remote_copy(
            src_ref=src, dst_ref=dst, send_sem=send.at[at], recv_sem=recv.at[at], device_id=to, device_id_type=MESH
        )

    barrier = pltpu.get_barrier_semaphore()
    everyone = [a_peer(r) for r in range(1, na)] + [group_peer(r) for r in range(1, group)] + [c_peer]
    for to in everyone:
        pl.semaphore_signal(barrier, inc=1, device_id=to, device_id_type=MESH)

    own_slot = kv.at[a, y, x]
    own = [
        pltpu.make_async_copy(src, dst, sem["own"].at[i])
        for i, (src, dst) in enumerate([
            (pos_ref, ids.at[0]), (doc_ref, ids.at[1]),
            (k_ref, kv.at[a, y, x, pl.ds(0, rows)]), (v_ref, kv.at[a, y, x, pl.ds(rows, rows)]),
            (q_ref, raw.at[0, c]), (g_ref, raw.at[1, c]),
        ])
    ]
    for one in own:
        one.start()

    own[0].wait()
    own[1].wait()
    pos_own = ids[0].astype(F32)
    doc_own = ids[1].astype(F32)
    coarse = jnp.floor(pos_own[:, 0:1] * (1.0 / 128.0))
    fields = [coarse, pos_own[:, 0:1] - coarse * 128.0]
    for d in range(docs):
        fields.append(jnp.sum(jnp.where(doc_own == d, 1.0, 0.0), axis=1, keepdims=True))
    field_ids = lax.broadcasted_iota(jnp.int32, (FACTS, 128), 0)
    table = jnp.zeros((FACTS, 128), F32)
    for f, one in enumerate(fields):
        table = jnp.where(field_ids == f, one, table)
    kv[a, y, x, 2 * rows :, :] = table.astype(BF16)

    pl.semaphore_wait(barrier, len(everyone))

    def a_copy(step):
        return copy(own_slot, own_slot, "a", step, a_peer(step))

    def group_copies(step):
        block = kv.at[xor(a, step, a_bits), y, x]
        return [copy(block, block, "g", step * group + r, group_peer(r)) for r in range(1, group)]

    def send_all(copies):
        for one in copies:
            one.start()

    own[2].wait()
    own[3].wait()
    first = [a_copy(r) for r in range(1, na)]
    send_all(first)
    send_all(group_copies(0))

    share = [copy(q_ref, raw.at[0, c], "qg", 0, c_peer), copy(g_ref, raw.at[1, c], "qg", 1, c_peer)]
    for one in share:
        one.start()

    spare = 128 - 2 * rows
    pieces = [pos_own, doc_own] + ([jnp.zeros((1, spare), F32)] if spare else [])
    info_q = sem["info_q"]
    info_q[c] = jnp.concatenate(pieces, axis=1)
    id_share = copy(info_q.at[c], info_q.at[c], "idq", 0, c_peer)
    id_share.start()

    def relay(step):
        a_copy(step).wait_recv()
        send_all(group_copies(step))

    def lay_out(core):
        base = core * lanes
        for h in range(heads):
            at = pl.ds(pl.multiple_of(base + h * rows, rows), rows)
            qs[at, :] = raw[0, core, :, h * 128 : (h + 1) * 128]
            gs[at, :] = raw[1, core, :, h * 128 : (h + 1) * 128]
        span = pl.ds(pl.multiple_of(base, lanes), lanes)
        qt[:, span] = jnp.transpose(qs[span, :])
        gt[:, span] = jnp.transpose(gs[span, :])

    for one in own[4:]:
        one.wait()
    lay_out(c)
    if na > 1:
        relay(1)
    for one in share + [id_share]:
        one.wait_recv()
    lay_out(1 - c)
    if na > 2:
        relay(2)
    both = [info_q[k] for k in range(CORES)]
    pos_q = jnp.concatenate([one[:, :rows] for one in both for _ in range(heads)], axis=1)
    doc_q = jnp.concatenate([one[:, rows : 2 * rows] for one in both for _ in range(heads)], axis=1)
    wide = CORES * lanes
    for k in range(CORES):
        stats[k, 0] = jnp.full((1, lanes), NEG_BIG, F32)
        stats[k, 1] = jnp.zeros((1, lanes), F32)
        stats[k, 2] = jnp.zeros((1, lanes), F32)
    stats_in, finals = sem["stats_in"], sem["finals"]

    def swap(k):
        return copy(stats.at[k], stats_in.at[k], "stat", k, c_peer)

    dqt[...] = jnp.zeros(dqt.shape, F32)

    tile = min(TILE, lanes)
    tiles = [slice(t, t + tile) for t in range(0, wide, tile)]
    row_ids = lax.broadcasted_iota(jnp.int32, (rows, tile), 0).astype(F32)

    def widen(row):
        return jnp.concatenate([row] * (tile // 128), axis=1)

    def chunk_of(step, which):
        part = slice(which * rows, (which + 1) * rows)
        return kv[xor(a, step, a_bits), :, :, part, :].reshape(group * rows, 128)

    def look(step, carry):
        @pl.when((step >= 1) & (step + 2 < na))
        def _():
            relay(step + 2)

        for one in group_copies(step):
            one.wait_recv()

        keys, values = chunk_of(step, 0), chunk_of(step, 1)
        at = xor(a, step, a_bits)
        tables = [kv[at, b // nx, b % nx, 2 * rows :, :].astype(F32) for b in range(group)]
        for cols in tiles:
            scores = dot(keys, qt[:, cols], 1, 0)
            k = cols.start // lanes
            local = slice(cols.start - k * lanes, cols.stop - k * lanes)
            old = stats[k, 0, :, local]
            high = old
            for b in range(group):
                row = lambda f: widen(tables[b][f : f + 1, :])
                upper = pos_q[:, cols] - row(0) * 128.0 - row(1)
                lower = jnp.zeros((1, tile), F32)
                for d in range(docs):
                    lower = lower + jnp.where(doc_q[:, cols] > d, row(2 + d), 0.0)
                seen = (row_ids >= lower) & (row_ids <= upper)
                part = jnp.where(seen, scores[b * rows : (b + 1) * rows, :] * scale, NEG_BIG)
                sbuf[step, b * rows : (b + 1) * rows, cols] = part
                high = jnp.maximum(high, jnp.max(part, axis=0, keepdims=True))
            dprobs = dot(values, gt[:, cols], 1, 0)
            dpbuf[step, :, cols] = dprobs
            fade = jnp.exp2(old - high)
            weights = jnp.exp2(sbuf[step, :, cols] - high)
            stats[k, 0, :, local] = high
            stats[k, 1, :, local] = stats[k, 1, :, local] * fade + jnp.sum(weights, axis=0, keepdims=True)
            stats[k, 2, :, local] = stats[k, 2, :, local] * fade + jnp.sum(weights * dprobs, axis=0, keepdims=True)
            if local.stop == lanes:

                @pl.when(step == na - 1)
                def _():
                    swap(k).start()

        return carry

    lax.fori_loop(0, na, look, 0)

    def finalize(k):
        swap(k).wait_recv()
        high = jnp.maximum(stats[k, 0], stats_in[k, 0])
        here, there = jnp.exp2(stats[k, 0] - high), jnp.exp2(stats_in[k, 0] - high)
        denom = stats[k, 1] * here + stats_in[k, 1] * there
        span = slice(k * lanes, (k + 1) * lanes)
        finals[0, :, span] = high + jnp.log2(denom)
        finals[1, :, span] = (stats[k, 2] * here + stats_in[k, 2] * there) / denom

    def sum_copies(step):
        found = []
        for r in range(1, group):
            yy, xx = group_place(r)
            at = step * group + r
            found.append(copy(g_out.at[step, :, yy, xx], g_in.at[at], "sum", at, group_peer(r)))
        return found

    def ra_copy(step):
        return copy(a_out.at[step], a_in.at[step], "ra", step, a_peer(step))

    def grads(step):
        keys_t = jnp.transpose(chunk_of(step, 0))
        for cols in tiles:
            if cols.start % lanes == 0:

                @pl.when(step == na - 1)
                def _():
                    finalize(cols.start // lanes)

            probs = jnp.exp2(sbuf[step, :, cols] - finals[0, :, cols])
            dscores = (probs * (dpbuf[step, :, cols] - finals[1, :, cols])).astype(BF16)
            sem["probs"][:, cols] = probs.astype(BF16)
            sem["dscores"][:, cols] = dscores
        dk = dot(sem["dscores"][...], qs[...], 1, 0)
        dv = dot(sem["probs"][...], gs[...], 1, 0)
        for which, one in enumerate((dk, dv)):
            one = one.reshape(SIDES, nx, rows, 128)
            g_out[step, which] = one.astype(BF16)
            acc[step, which] = one
        send_all(sum_copies(step))
        for k in range(CORES):
            dqt[k] += dot(keys_t, sem["dscores"][:, k * lanes : (k + 1) * lanes], 1, 0)

    def second(step):
        total = acc[step, :, y, x]
        for r, one in enumerate(sum_copies(step)):
            one.wait_recv()
            total = total + g_in[step * group + r + 1].astype(F32)
        a_own[step] = total

        @pl.when(step > 0)
        def _():
            a_out[step] = total.astype(BF16)
            ra_copy(step).start()

    def turn(i, carry):
        grads(na - 1 - i)

        @pl.when(i >= LAG)
        def _():
            second(na - 1 - i + LAG)

        return carry

    lax.fori_loop(0, na, turn, 0)
    swap_dq = copy(dqt.at[1 - c], dq_in, "dq", 0, c_peer)
    swap_dq.start()

    for step in range(min(LAG, na) - 1, 0, -1):
        second(step)
    swap_dq.wait_recv()
    dq = jnp.transpose(dqt[c] + dq_in[...]) * inv_root
    for h in range(heads):
        dq_ref[:, h * 128 : (h + 1) * 128] = dq[h * rows : (h + 1) * rows, :]
    second(0)

    for one in first + share + [id_share, swap(0), swap(1), swap_dq]:
        one.wait_send()

    def sent(step, carry):
        @pl.when(step > 0)
        def _():
            ra_copy(step).wait_send()

        for one in group_copies(step) + sum_copies(step):
            one.wait_send()
        return carry

    lax.fori_loop(0, na, sent, 0)

    def collect(step, carry):
        ra_copy(step).wait_recv()
        return carry + a_in[step].astype(F32)

    done = lax.fori_loop(1, na, collect, a_own[0])
    dk_ref[...] = done[0] * inv_root
    dv_ref[...] = done[1]


def hand_over(*refs):
    count = (len(refs) - 1) // 2
    moves = [pltpu.make_async_copy(refs[i], refs[count + i], refs[-1].at[i]) for i in range(count)]
    for one in moves:
        one.start()
    for one in moves:
        one.wait()


def on_device(queries, key_vecs, value_vecs, out_grad, positions, documents):
    nx = lax.axis_size("head")
    na = lax.axis_size("ctx") // (CORES * SIDES)
    rows, width = queries.shape
    heads = width // 128
    seq = rows * nx * na * CORES * SIDES
    docs = max(2, seq // 1024)
    lanes, group = heads * rows, SIDES * nx
    chunk = group * rows
    wide = CORES * lanes
    dma = pltpu.SemaphoreType.DMA
    vmem = pltpu.VMEM
    copies = {
        "a": na, "g": na * group, "idq": 1, "qg": 2, "stat": CORES,
        "sum": na * group, "ra": na, "dq": 1,
    }
    names, tail = [], []
    for name, count in copies.items():
        names += ["s_" + name, "r_" + name]
        tail += [dma((count,)), dma((count,))]
    names += ["own", "info_q", "stats_in", "finals", "probs", "dscores"]
    tail += [dma((6,)), vmem((CORES, 1, 128), F32), vmem((CORES, 3, 1, lanes), F32), vmem((2, 1, wide), F32)]
    tail += [vmem((chunk, wide), BF16), vmem((chunk, wide), BF16)]
    scratch = [
        vmem((2, CORES, rows, width), BF16),
        vmem((wide, 128), BF16),
        vmem((wide, 128), BF16),
        vmem((128, wide), BF16),
        vmem((128, wide), BF16),
        vmem((na, SIDES, nx, 2 * rows + FACTS, 128), BF16),
        vmem((2, 1, rows), jnp.int32),
        vmem((na, chunk, wide), F32),
        vmem((na, chunk, wide), F32),
        vmem((CORES, 3, 1, lanes), F32),
        vmem((CORES, 128, lanes), F32),
        vmem((128, lanes), F32),
        vmem((na, 2, SIDES, nx, rows, 128), F32),
        vmem((na, 2, SIDES, nx, rows, 128), BF16),
        vmem((na * group, 2, rows, 128), BF16),
        vmem((na, 2, rows, 128), BF16),
        vmem((na, 2, rows, 128), BF16),
        vmem((na, 2, rows, 128), F32),
    ] + tail
    cfg = (nx, na, rows, heads, docs, names)
    far = pl.BlockSpec(memory_space=pltpu.HBM)
    pairs = lanes * seq
    shapes = (
        jax.ShapeDtypeStruct((rows, width), F32),
        jax.ShapeDtypeStruct((rows, 128), F32),
        jax.ShapeDtypeStruct((rows, 128), F32),
    )
    near = pl.BlockSpec(memory_space=pltpu.VMEM)
    found = pl.pallas_call(
        functools.partial(kernel, cfg),
        out_shape=tuple(pltpu.VMEM(one.shape, one.dtype) for one in shapes),
        in_specs=[far] * 6,
        out_specs=(near, near, near),
        scratch_shapes=scratch,
        compiler_params=pltpu.CompilerParams(
            collective_id=0, has_side_effects=True, vmem_limit_bytes=63 * 1024 * 1024
        ),
        cost_estimate=pl.CostEstimate(
            flops=10 * pairs * 128, bytes_accessed=rows * width * 8, transcendentals=2 * pairs
        ),
    )(queries, key_vecs, value_vecs, out_grad, positions.reshape(1, rows), documents.reshape(1, rows))
    return pl.pallas_call(
        hand_over,
        out_shape=shapes,
        in_specs=[pl.BlockSpec(memory_space=pltpu.VMEM)] * 3,
        out_specs=(far, far, far),
        scratch_shapes=[dma((3,))],
        compiler_params=pltpu.CompilerParams(vmem_limit_bytes=1024 * 1024),
    )(*found)


def solution(mesh):
    tokens = P(("head", "ctx"), None)
    ids = P(("head", "ctx"))
    return jax.shard_map(
        on_device,
        mesh=mesh,
        in_specs=(tokens, tokens, tokens, tokens, ids, ids),
        out_specs=(tokens, tokens, tokens),
        check_vma=False,
    )
```
